256 devices in a mesh: prow: 8 (over z), pcol: 32 (over x, y, core).
Axes of the slice: x: 4, y: 4, z: 8, core: 2. Of those that a mesh axis runs over, the one named last changes fastest.
Arguments:
- hamiltonian: float32 [8, 2048, 2, 8192], P(None, 'prow', None, 'pcol'), may hold values from -7 to 7, as said below
Outputs:
- reduced: float32 [8, 2048, 2, 8192], P(None, 'prow', None, 'pcol')
The draws below stay inside these ranges and needn't reach their ends.
Inputs may be any that keep to these rules, and one draw needn't show every extreme that they name: `hamiltonian`: symmetric; the panel A[256:, :256] has full column rank and I + K^T is invertible.
All inputs are finite; a program needn't handle non-finite values.
Results may differ from the reference program's by a relative error of at most 0.00011.
Values sent between devices are 32-bit elements; how exact they have to be, the bound alone decides.
No kernel may reach another device: no remote copies, remote signals or barrier semaphores. Data moves between devices by JAX's collectives and lax.ppermute only.
A program may use at most 128 MiB of HBM per device.

```python
import math
import jax
import jax.numpy as jnp
from jax import lax

N = 16384
NB = 256
N_PROW = 8
N_PCOL = 32


def draw_hamiltonian(key, part):
    key = jax.random.fold_in(key, 7)
    raw = jnp.clip(jax.random.normal(key, (N, N), jnp.float32), -4.5, 4.5)
    rows = jnp.arange(N, dtype=jnp.int32)[:, None]
    cols = jnp.arange(N, dtype=jnp.int32)[None, :]
    row_blk = rows // NB
    col_blk = cols // NB
    near = 0.25 / math.sqrt(NB)
    far = 1.0 / math.sqrt(N - 2 * NB)
    paired = (raw + raw.T) * 0.70710677
    lower_panel = raw * jnp.where(row_blk == 1, near, far) + jnp.where(rows - NB == cols, 1.0, 0.0)
    upper_panel = raw.T * jnp.where(col_blk == 1, near, far) + jnp.where(cols - NB == rows, 1.0, 0.0)
    whole = jnp.where((col_blk == 0) & (row_blk >= 1), lower_panel, jnp.where((row_blk == 0) & (col_blk >= 1), upper_panel, paired))
    return whole.reshape(N // (NB * N_PROW), N_PROW * NB, N // (NB * N_PCOL), N_PCOL * NB)


def setup_inputs(seed: int = 0) -> dict:
    seeds = jax.random.split(jax.random.key(seed), 2)
    hamiltonian = draw_hamiltonian(jax.random.fold_in(seeds[1], 71), 0)
    return dict(hamiltonian=hamiltonian)


def small_inverse(k_top, ident):
    hp = lax.Precision.HIGHEST
    matrix = ident + k_top.T
    normal = jnp.dot(matrix.T.astype(jnp.float32), matrix.astype(jnp.float32), precision=hp, preferred_element_type=jnp.float32)
    factor = jnp.linalg.cholesky(normal)
    return jax.scipy.linalg.cho_solve((factor, True), matrix.T)

def reference(hamiltonian):
    hp = lax.Precision.HIGHEST
    full = hamiltonian.reshape(N, N)
    panel = full[NB:, :NB]
    trail = full[NB:, NB:]
    ident = jnp.eye(NB, dtype=jnp.float32)
    gram = jnp.dot(panel.T.astype(jnp.float32), panel.astype(jnp.float32), precision=hp, preferred_element_type=jnp.float32)
    lower = jnp.linalg.cholesky(gram)
    basis = jax.scipy.linalg.solve_triangular(lower, panel.T, lower=True).T
    mixer = small_inverse(basis[:NB], ident)
    vectors = basis.at[:NB].add(ident)
    applied = jnp.dot(trail.astype(jnp.float32), vectors.astype(jnp.float32), precision=hp, preferred_element_type=jnp.float32)
    proj = jnp.dot(vectors.T.astype(jnp.float32), applied.astype(jnp.float32), precision=hp, preferred_element_type=jnp.float32)
    core = jnp.dot(jnp.dot(mixer.T, proj, precision=hp), mixer, precision=hp)
    shifted = jnp.dot(applied.astype(jnp.float32), mixer.astype(jnp.float32), precision=hp, preferred_element_type=jnp.float32)
    weights = shifted - 0.5 * jnp.dot(vectors.astype(jnp.float32), core.astype(jnp.float32), precision=hp, preferred_element_type=jnp.float32)
    new_trail = trail - jnp.dot(vectors, weights.T, precision=hp) - jnp.dot(weights, vectors.T, precision=hp)
    band = jnp.zeros((N - NB, NB), jnp.float32).at[:NB].set(-lower.T)
    top = jnp.concatenate([full[:NB, :NB], band.T], axis=1)
    bottom = jnp.concatenate([band, new_trail], axis=1)
    result = jnp.concatenate([top, bottom], axis=0)
    return result.reshape(hamiltonian.shape)
```

```python
import jax
import jax.numpy as jnp
from jax import lax
from jax.sharding import PartitionSpec as P

HP = lax.Precision.HIGHEST
XS, YS, CORES = 4, 4, 2
CHIPS = XS * YS
PLANE = [[q * CORES + k for q in range(CHIPS)] for k in range(CORES)]
YLINE = [[(x * YS + y) * CORES + k for y in range(YS)] for x in range(XS) for k in range(CORES)]
SWAP = [(i, i ^ 1) for i in range(CHIPS * CORES)]


def mm(a, b):
    return jnp.dot(a, b, precision=HP, preferred_element_type=jnp.float32)


def mm_tn(a, b):
    return lax.dot_general(a, b, (((0,), (0,)), ((), ())), precision=HP, preferred_element_type=jnp.float32)


def mm_nt(a, b):
    return lax.dot_general(a, b, (((1,), (1,)), ((), ())), precision=HP, preferred_element_type=jnp.float32)


def share(piece, axis, count, groups=None):
    copies = jnp.broadcast_to(piece[None], (count,) + piece.shape)
    return lax.all_to_all(copies, axis, 0, 0, axis_index_groups=groups)


def both_halves(half, core):
    other = lax.ppermute(half, "pcol", SWAP)
    first = core == 0
    return jnp.stack([jnp.where(first, half, other), jnp.where(first, other, half)])


def small_math(gram, top, ident):
    lower = jnp.linalg.cholesky(gram)
    inv = jax.scipy.linalg.solve_triangular(lower, ident, lower=True)
    matrix = ident + mm_nt(inv, top)
    normal = mm_tn(matrix, matrix)
    factor = jnp.linalg.cholesky(normal)
    mixer = jax.scipy.linalg.cho_solve((factor, True), matrix.T)
    return lower, inv, mixer


def body(hamiltonian):
    nl, nb, nm, _ = hamiltonian.shape
    nz = lax.axis_size("prow")
    prow = lax.axis_index("prow")
    pcol = lax.axis_index("pcol")
    core = pcol % CORES
    yat = (pcol // CORES) % YS
    row_block = jnp.arange(nl, dtype=jnp.int32) * nz + prow
    col_block = jnp.arange(nm, dtype=jnp.int32) * (CHIPS * CORES) + pcol
    ident = jnp.eye(nb, dtype=jnp.float32)
    sub = nb // (CHIPS * CORES)
    matrix = hamiltonian.reshape(nl * nb, nm * nb)

    top_row = jnp.where((col_block >= 1)[None, :, None] & (prow == 0), hamiltonian[0], 0.0)
    p_cols_t = lax.psum(top_row, "prow").reshape(nb, nm * nb)

    panel = jnp.where((row_block >= 1)[:, None, None], hamiltonian[:, :, 0, :], 0.0)
    flat = panel.reshape(nl * nb, nb)
    gram_part = mm_tn(flat, flat)
    packet = jnp.concatenate(
        [
            panel.reshape(nl, CORES, CHIPS, sub, nb).transpose(1, 2, 0, 3, 4),
            gram_part.reshape(CORES, CHIPS, 1, sub, nb),
        ],
        axis=2,
    )
    given = lax.ppermute(packet[1], "pcol", [(0, 1)])
    outgoing = jnp.where(pcol == 0, packet[0], given)
    mine = lax.all_to_all(outgoing, "pcol", 0, 0, axis_index_groups=PLANE)[0]
    stacked = share(jnp.stack([mine[nl], mine[0]]), "prow", nz)
    gram_piece = jnp.sum(stacked[:, 0], axis=0)
    top_piece = stacked[1, 1]
    half = share(
        jnp.concatenate([mine[:nl], gram_piece[None], top_piece[None]]), "pcol", CHIPS, PLANE
    )
    whole = both_halves(half, core)
    p_rows = whole[:, :, :nl].transpose(2, 0, 1, 3, 4).reshape(nl * nb, nb)
    gram = whole[:, :, nl].reshape(nb, nb)
    top = whole[:, :, nl + 1].reshape(nb, nb)

    lower, inv, mixer = small_math(gram, top, ident)

    y_rows = mm_nt(p_rows, inv).reshape(nl, nb, nb)
    y_rows = y_rows + jnp.where((row_block == 1)[:, None, None], ident[None], 0.0)
    y_rows = y_rows.reshape(nl * nb, nb)
    y_cols = mm_nt(p_cols_t.T, inv).reshape(nm, nb, nb)
    y_cols = y_cols + jnp.where((col_block == 1)[:, None, None], ident[None], 0.0)
    y_cols = y_cols.reshape(nm * nb, nb)

    live = jnp.where((row_block >= 1)[:, None, None], y_rows.reshape(nl, nb, nb), 0.0)
    part = mm_tn(matrix, live.reshape(nl * nb, nb))
    part = jnp.where((col_block >= 1)[:, None, None], part.reshape(nm, nb, nb), 0.0)
    piece = jnp.sum(
        lax.all_to_all(part.reshape(nz, nm * nb // nz, nb), "prow", 0, 0), axis=0
    )
    ay_cols = share(piece, "prow", nz).reshape(nm * nb, nb)
    proj_part = mm_tn(y_cols, ay_cols)

    hb = nb // CORES
    qb = hb // YS
    pack = jnp.concatenate(
        [ay_cols.reshape(nm, CORES, hb, nb), proj_part.reshape(1, CORES, hb, nb)]
    ).transpose(1, 0, 2, 3)
    first = core == 0
    keep = jnp.where(first, pack[0], pack[1])
    got = lax.ppermute(jnp.where(first, pack[1], pack[0]), "pcol", SWAP)
    ay_half = jnp.where(core == prow % CORES, keep[:nm], got[:nm])
    proj_half = keep[nm:] + got[nm:]
    lines = jnp.concatenate([ay_half, proj_half]).reshape(nm + 1, YS, qb, nb).transpose(1, 0, 2, 3)
    lines = lax.all_to_all(lines, "pcol", 0, 0, axis_index_groups=YLINE)
    ay_piece = lax.dynamic_index_in_dim(lines[:, :nm], prow // CORES, 0, keepdims=False)
    proj_piece = jnp.sum(lines[:, nm:], axis=0)
    half = share(jnp.concatenate([ay_piece, proj_piece]), "pcol", CHIPS, PLANE)
    half = half.reshape(XS, YS, nm + 1, qb, nb)
    half = jnp.concatenate(
        [
            half[:, :, :nm].transpose(2, 0, 1, 3, 4).reshape(nm * XS, hb, nb),
            jnp.sum(half[:, :, nm], axis=0).reshape(1, hb, nb),
        ]
    )
    whole = both_halves(half, core).transpose(1, 0, 2, 3)
    ay_rows = whole[: nm * XS].reshape(nl * nb, nb)
    proj = whole[nm * XS].reshape(nb, nb)

    core_matrix = mm(mm_tn(mixer, proj), mixer)
    w_cols = mm(ay_cols, mixer) - mm(y_cols, core_matrix)
    v_cols = mm_nt(y_cols, mixer)
    live = jnp.where((row_block >= 1)[:, None, None], y_rows.reshape(nl, nb, nb), 0.0)
    left = jnp.concatenate([live.reshape(nl * nb, nb), ay_rows], axis=1)
    right = jnp.concatenate([w_cols, v_cols], axis=1)
    updated = (matrix - mm_nt(left, right)).reshape(nl, nb, nm, nb)
    band_col = jnp.where((row_block == 1)[:, None, None], -lower.T[None], 0.0)
    in_col = (col_block == 0)[None, None, :, None] & (row_block >= 1)[:, None, None, None]
    updated = jnp.where(in_col, band_col[:, :, None, :], updated)
    band_row = jnp.where((col_block == 1)[None, :, None], -lower[:, None, :], 0.0)
    in_row = (row_block == 0)[:, None, None, None] & (col_block >= 1)[None, None, :, None]
    return jnp.where(in_row, band_row[None], updated)


def solution(mesh):
    return jax.shard_map(
        body,
        mesh=mesh,
        in_specs=(P(None, "prow", None, "pcol"),),
        out_specs=P(None, "prow", None, "pcol"),
        check_vma=False,
    )
```

```python
import functools
import jax
import jax.numpy as jnp
from jax import lax
from jax.experimental import pallas as pl
from jax.experimental.pallas import tpu as pltpu
from jax.sharding import PartitionSpec as P

HP = lax.Precision.HIGHEST
XS, YS, CORES = 4, 4, 2
CHIPS = XS * YS
LANES = 128
BASE = 64
GROUP = 8
PLANE = [[q * CORES + k for q in range(CHIPS)] for k in range(CORES)]
YLINE = [[(x * YS + y) * CORES + k for y in range(YS)] for x in range(XS) for k in range(CORES)]
SWAP = [(i, i ^ 1) for i in range(CHIPS * CORES)]
VMEM = pl.BlockSpec(memory_space=pltpu.VMEM)
SMEM = pl.BlockSpec(memory_space=pltpu.SMEM)


def mm(a, b):
    return jnp.dot(a, b, precision=HP, preferred_element_type=jnp.float32)


def mm_tn(a, b):
    return lax.dot_general(a, b, (((0,), (0,)), ((), ())), precision=HP, preferred_element_type=jnp.float32)


def mm_nt(a, b):
    return lax.dot_general(a, b, (((1,), (1,)), ((), ())), precision=HP, preferred_element_type=jnp.float32)


def eliminate(block, jordan):
    n = block.shape[0]
    eye = (lax.broadcasted_iota(jnp.int32, (n, n), 0) == lax.broadcasted_iota(jnp.int32, (n, n), 1))
    wide = jnp.concatenate([block, eye.astype(jnp.float32)], axis=1)
    shape = (GROUP, 2 * n)
    groups = n // GROUP
    at = lax.broadcasted_iota(jnp.int32, shape, 0)
    w = [wide[g * GROUP : (g + 1) * GROUP] for g in range(groups)]
    for p in range(groups):
        live = [g for g in range(groups) if jordan or g >= p]
        cols = {
            g: [
                jnp.broadcast_to(w[g][:, p * GROUP + b : p * GROUP + b + 1], shape)
                for b in range(GROUP)
            ]
            for g in live
        }
        for a in range(GROUP):
            inv = 1.0 / cols[p][a][a : a + 1]
            row = w[p][a : a + 1]
            heads = [cols[p][b][a : a + 1] for b in range(GROUP)]
            for g in live:
                m = cols[g][a] * inv
                if g == p:
                    m = jnp.where(at != a if jordan else at > a, m, 0.0)
                for b in range(a + 1, GROUP):
                    cols[g][b] = cols[g][b] - m * heads[b]
                w[g] = w[g] - m * row
    return jnp.concatenate(w, axis=0)


def diagonal(wide):
    n = wide.shape[0]
    shape = wide.shape
    eye = lax.broadcasted_iota(jnp.int32, shape, 0) == lax.broadcasted_iota(jnp.int32, shape, 1)
    return jnp.sum(jnp.where(eye, wide, 0.0), axis=1, keepdims=True)


def factor(a):
    n = a.shape[0]
    if n <= BASE:
        wide = eliminate(a, False)
        wide = wide * (1.0 / jnp.sqrt(diagonal(wide)))
        left = wide[:, :n]
        upper = lax.broadcasted_iota(jnp.int32, (n, n), 0) <= lax.broadcasted_iota(jnp.int32, (n, n), 1)
        return jnp.where(upper, left, 0.0), wide[:, n:]
    h = n // 2
    u11, i11 = factor(a[:h, :h])
    u12 = mm(i11, a[:h, h:])
    u22, i22 = factor(a[h:, h:] - mm_tn(u12, u12))
    i21 = -mm(i22, mm_tn(u12, i11))
    zero = jnp.zeros((h, h), jnp.float32)
    upper = jnp.concatenate([jnp.concatenate([u11, u12], 1), jnp.concatenate([zero, u22], 1)], 0)
    inv = jnp.concatenate([jnp.concatenate([i11, zero], 1), jnp.concatenate([i21, i22], 1)], 0)
    return upper, inv


def inverse(a):
    n = a.shape[0]
    if n <= BASE:
        wide = eliminate(a, True)
        return (wide * (1.0 / diagonal(wide)))[:, n:]
    h = n // 2
    i11 = inverse(a[:h, :h])
    x = mm(i11, a[:h, h:])
    y = mm(a[h:, :h], i11)
    s = inverse(a[h:, h:] - mm(a[h:, :h], x))
    xs = mm(x, s)
    top = jnp.concatenate([i11 + mm(xs, y), -xs], 1)
    return jnp.concatenate([top, jnp.concatenate([-mm(s, y), s], 1)], 0)


def split(a):
    high = a.astype(jnp.bfloat16)
    return high, (a - high.astype(jnp.float32)).astype(jnp.bfloat16)


def dot3(a, b, dims):
    one = functools.partial(
        lax.dot_general, dimension_numbers=(dims, ((), ())), preferred_element_type=jnp.float32
    )
    return one(a[0], b[0]) + (one(a[0], b[1]) + one(a[1], b[0]))


def identity(n):
    rows = lax.broadcasted_iota(jnp.int32, (n, n), 0)
    return (rows == lax.broadcasted_iota(jnp.int32, (n, n), 1)).astype(jnp.float32)


def tile(ref, m, t, nm, nt):
    return ref[pl.ds(t * nm + m, ref.shape[0] // (nm * nt), stride=nm * nt), :]


def in_order(at_ref, own, other):
    first = at_ref[2] == 0
    return jnp.concatenate([jnp.where(first, own, other), jnp.where(first, other, own)], axis=0)


def rows_of(ref):
    return ref[...].reshape(-1, ref.shape[-1])


def pack_kernel(nm, nt, at_ref, x_ref, packet_ref, gram_ref):
    step = pl.program_id(0)
    last = pl.num_programs(0) - 1

    @pl.when(step < last)
    def _():
        panel = jnp.concatenate([tile(x_ref, 0, t, nm, nt) for t in range(nt)], axis=1)
        panel = jnp.where((step == 0) & (at_ref[0] == 0), 0.0, panel)
        packet_ref[...] = panel.reshape(packet_ref.shape)
        more = mm_tn(panel, panel)

        @pl.when(step == 0)
        def _():
            gram_ref[...] = more

        @pl.when(step > 0)
        def _():
            gram_ref[...] += more

    @pl.when(step == last)
    def _():
        packet_ref[...] = gram_ref[...].reshape(packet_ref.shape)


def factor_kernel(at_ref, own_ref, other_ref, upper_ref, inv_ref, inv_t_ref):
    upper, inv = factor(in_order(at_ref, rows_of(own_ref), rows_of(other_ref)))
    upper_ref[...] = upper
    inv_ref[...] = inv
    inv_t_ref[...] = inv.T


def mixer_kernel(at_ref, own_ref, other_ref, inv_ref, after_ref, mixer_ref):
    top = in_order(at_ref, rows_of(own_ref), rows_of(other_ref))
    mixer_ref[...] = inverse(identity(top.shape[0]) + mm_nt(inv_ref[...], top))


def apply_kernel(nm, nt, at_ref, x_ref, own_ref, other_ref, inv_t_ref, y_ref, part_ref, sum_ref):
    step = pl.program_id(0)
    nb = inv_t_ref.shape[0]
    y = mm(in_order(at_ref, rows_of(own_ref), rows_of(other_ref)), inv_t_ref[...])
    y += jnp.where((step == 0) & (at_ref[0] == 1), identity(nb), 0.0)
    y_ref[0] = y
    block = jnp.concatenate(
        [tile(x_ref, m, t, nm, nt) for m in range(nm) for t in range(nt)], axis=1
    )
    more = dot3(split(y.T), split(block), ((1,), (0,)))

    @pl.when(step == 0)
    def _():
        sum_ref[...] = more

    @pl.when(step > 0)
    def _():
        sum_ref[...] += more

    @pl.when(step == pl.num_programs(0) - 1)
    def _():
        total = sum_ref[...].T
        part_ref[:nb] = jnp.where(at_ref[1] == 0, 0.0, total[:nb])
        part_ref[nb:] = total[nb:]


def cols_kernel(nm, nt, at_ref, top_ref, inv_ref, y_ref):
    nb = inv_ref.shape[0]
    parts = [
        mm(inv_ref[...], jnp.concatenate([tile(top_ref, m, t, nm, nt) for t in range(nt)], axis=1))
        for m in range(nm)
    ]
    parts[0] += jnp.where(at_ref[1] == 1, identity(nb), 0.0)
    y_ref[...] = jnp.concatenate(parts, axis=1)


def proj_kernel(at_ref, y_ref, ay_ref, keep_ref, send_ref):
    nb = y_ref.shape[0]
    hb = nb // CORES
    ay = ay_ref[...]
    proj = mm(y_ref[...], ay)
    parts = [ay[i * nb : (i + 1) * nb] for i in range(ay.shape[0] // nb)] + [proj]
    first = at_ref[2] == 0
    for i, p in enumerate(parts):
        keep_ref[i] = jnp.where(first, p[:hb], p[hb:])
        send_ref[i] = jnp.where(first, p[hb:], p[:hb])


def sides_kernel(mixer_ref, y_ref, ay_ref, z_ref, v_ref):
    mixer = mixer_ref[...]
    z_ref[...] = lax.dot_general(
        mixer, ay_ref[...], (((0,), (1,)), ((), ())), precision=HP, preferred_element_type=jnp.float32
    )
    v_ref[...] = mm(mixer, y_ref[...])


def update_kernel(
    nm, nt, at_ref, x_ref, left_ref, own_ref, other_ref, own_proj_ref, other_proj_ref,
    mixer_ref, y_ref, z_ref, v_ref, upper_ref, out_ref, high_ref, low_ref,
):
    step = pl.program_id(0)
    nb = mixer_ref.shape[0]

    @pl.when(step == 0)
    def _():
        halves = [
            jnp.sum(ref[...].reshape(XS, nb // CORES, nb), axis=0)
            for ref in (own_proj_ref, other_proj_ref)
        ]
        mixer = mixer_ref[...]
        core = mm(mm_tn(mixer, in_order(at_ref, *halves)), mixer)
        w = split(z_ref[...] - mm_tn(core, y_ref[...]))
        v = split(v_ref[...])
        for i, ref in enumerate((high_ref, low_ref)):
            ref[:nb] = w[i]
            ref[nb:] = v[i]

    ay = in_order(at_ref, rows_of(own_ref), rows_of(other_ref))
    left = split(jnp.concatenate([left_ref[0], ay], axis=1))
    change = dot3(left, (high_ref[...], low_ref[...]), ((1,), (0,)))
    rows = nb
    for m in range(nm):
        for t in range(nt):
            at = m * nb + t * LANES
            out_ref[pl.ds(t * nm + m, rows, stride=nm * nt), :] = (
                tile(x_ref, m, t, nm, nt) - change[:, at : at + LANES]
            )

    @pl.when(at_ref[1] == 0)
    def _():
        keep = (step == 0) & (at_ref[0] == 0)
        band = jnp.where((step == 0) & (at_ref[0] == 1), -upper_ref[...], 0.0)
        for t in range(nt):
            old = tile(x_ref, 0, t, nm, nt)
            out_ref[pl.ds(t * nm, rows, stride=nm * nt), :] = jnp.where(
                keep, old, band[:, t * LANES : (t + 1) * LANES]
            )

    @pl.when((step == 0) & (at_ref[0] == 0))
    def _():
        band = jnp.where(at_ref[1] == 1, -upper_ref[...].T, 0.0)
        for m in range(nm):
            for t in range(nt):
                new = band[:, t * LANES : (t + 1) * LANES] if m == 0 else jnp.zeros((rows, LANES))
                if m == 0:
                    new = jnp.where(at_ref[1] == 0, tile(x_ref, m, t, nm, nt), new)
                out_ref[pl.ds(t * nm + m, rows, stride=nm * nt), :] = new


def call(kernel, outs, ins, grid=(), flops=0, moved=1 << 20, scratch=()):
    return pl.pallas_call(
        kernel,
        grid=grid,
        out_shape=[jax.ShapeDtypeStruct(s, jnp.float32) for s, _ in outs],
        in_specs=ins,
        out_specs=[spec for _, spec in outs],
        scratch_shapes=list(scratch),
        compiler_params=pltpu.CompilerParams(vmem_limit_bytes=40 << 20),
        cost_estimate=pl.CostEstimate(flops=flops, bytes_accessed=moved, transcendentals=0),
    )


def share(piece, axis, count, groups=None):
    copies = jnp.broadcast_to(piece[None], (count,) + piece.shape)
    return lax.all_to_all(copies, axis, 0, 0, axis_index_groups=groups)


def doubled(block, reach, nz):
    pairs = [(i, i + reach) for i in range(0, nz, 2 * reach)]
    return block + lax.ppermute(block, "prow", pairs)


def body(hamiltonian):
    nl, nb, nm, _ = hamiltonian.shape
    nt = nb // LANES
    nz = lax.axis_size("prow")
    prow = lax.axis_index("prow")
    pcol = lax.axis_index("pcol")
    core = pcol % CORES
    at = jnp.stack([prow, pcol, core]).astype(jnp.int32)
    sub = nb // (CHIPS * CORES)
    hb = nb // CORES
    qb = hb // YS
    nc = nm * nb
    square, wide, tall = (nb, nb), (nb, nc), (nc, nb)

    x = hamiltonian.reshape(nl, nb, nm, nt, LANES).transpose(0, 1, 3, 2, 4)
    x = x.reshape(nl * nb * nt * nm, LANES)
    x_rows = nb * nt * nm
    x_spec = pl.BlockSpec((x_rows, LANES), lambda l: (l, 0))

    first_rows = x[:x_rows].reshape(nb * nt, nm, LANES)
    live = (jnp.arange(nm, dtype=jnp.int32) * (CHIPS * CORES) + pcol >= 1) & (prow == 0)
    p_cols = jnp.where(live[None, :, None], first_rows, 0.0).reshape(x_rows, LANES)

    packet = call(
        functools.partial(pack_kernel, nm, nt),
        [((CORES, CHIPS, nl + 1, sub, nb),
          pl.BlockSpec((CORES, CHIPS, 1, sub, nb), lambda l: (0, 0, l, 0, 0)))],
        [SMEM, pl.BlockSpec((x_rows, LANES), lambda l: (jnp.minimum(l, nl - 1), 0))],
        grid=(nl + 1,),
        flops=12 * nl * nb**3,
        moved=6 << 20,
        scratch=[pltpu.VMEM(square, jnp.float32)],
    )(at, x)[0]
    given = lax.ppermute(packet[1], "pcol", [(0, 1)])
    outgoing = jnp.where(pcol == 0, packet[0], given)
    mine = lax.all_to_all(outgoing, "pcol", 0, 0, axis_index_groups=PLANE)[0]
    p_cols, mine = lax.optimization_barrier((doubled(p_cols, 4, nz), mine))
    stacked = share(jnp.stack([mine[nl], mine[0]]), "prow", nz)
    p_cols, stacked = lax.optimization_barrier((doubled(p_cols, 2, nz), stacked))
    gram_piece = jnp.sum(stacked[:, 0], axis=0)
    own = share(
        jnp.concatenate([mine[:nl], gram_piece[None], stacked[1, 1][None]]), "pcol", CHIPS, PLANE
    )
    p_cols, own = lax.optimization_barrier((doubled(p_cols, 1, nz), own))
    other = lax.ppermute(own, "pcol", SWAP)

    def chunk(index):
        return pl.BlockSpec((CHIPS, 1, sub, nb), index)

    gram_spec = chunk(lambda l: (0, nl, 0, 0))
    upper, inv, inv_t = call(
        factor_kernel, [(square, VMEM)] * 3, [SMEM, gram_spec, gram_spec], grid=(1,), flops=10**10
    )(at, own, other)

    whole = lambda shape: pl.BlockSpec(shape, lambda l: (0,) * len(shape))
    row_spec = chunk(lambda l: (0, l, 0, 0))
    y_rows, part = call(
        functools.partial(apply_kernel, nm, nt),
        [((nl, nb, nb), pl.BlockSpec((1, nb, nb), lambda l: (l, 0, 0))), (tall, whole(tall))],
        [SMEM, x_spec, row_spec, row_spec, whole(square)],
        grid=(nl,),
        flops=12 * nl * nb**2 * (nb + nc),
        moved=9 << 20,
        scratch=[pltpu.VMEM(wide, jnp.float32)],
    )(at, x, own, other, inv_t)
    top_spec = chunk(lambda l: (0, nl + 1, 0, 0))
    mixer = call(
        mixer_kernel,
        [(square, VMEM)],
        [SMEM, top_spec, top_spec, VMEM, pl.BlockSpec(memory_space=pl.ANY)],
        grid=(1,),
        flops=10**10,
    )(at, own, other, inv, part)[0]
    y_cols = call(
        functools.partial(cols_kernel, nm, nt), [(wide, VMEM)], [SMEM, VMEM, VMEM], flops=10**9
    )(at, p_cols, inv)[0]
    parts = lax.all_to_all(part.reshape(nz, nc // nz, nb), "prow", 0, 0)
    parts, mixer = lax.optimization_barrier((parts, mixer))
    ay_cols = share(jnp.sum(parts, axis=0), "prow", nz).reshape(nc, nb)
    ay_cols, y_cols = lax.optimization_barrier((ay_cols, y_cols))

    half_shape = (nm + 1, hb, nb)
    keep, send = call(proj_kernel, [(half_shape, VMEM)] * 2, [SMEM, VMEM, VMEM], flops=10**9)(
        at, y_cols, ay_cols
    )
    got = lax.ppermute(send, "pcol", SWAP)
    lines = jnp.concatenate([jnp.where(core == prow % CORES, keep[:nm], got[:nm]), keep[nm:] + got[nm:]])
    lines = lines.reshape(nm + 1, YS, qb, nb).transpose(1, 0, 2, 3)
    lines = lax.all_to_all(lines, "pcol", 0, 0, axis_index_groups=YLINE)
    z_cols, v_cols = call(sides_kernel, [(wide, VMEM)] * 2, [VMEM] * 3, flops=3 * 10**9)(
        mixer, y_cols, ay_cols
    )
    lines, z_cols, v_cols = lax.optimization_barrier((lines, z_cols, v_cols))
    ay_piece = lax.dynamic_index_in_dim(lines[:, :nm], prow // CORES, 0, keepdims=False)
    half = share(
        jnp.concatenate([ay_piece, jnp.sum(lines[:, nm:], axis=0)]), "pcol", CHIPS, PLANE
    ).reshape(XS, YS, nm + 1, qb, nb)
    other_half = lax.ppermute(half, "pcol", SWAP)
    ay_spec = pl.BlockSpec((1, YS, 1, qb, nb), lambda l: (l % XS, 0, l // XS, 0, 0))
    proj_spec = pl.BlockSpec((XS, YS, 1, qb, nb), lambda l: (0, 0, nm, 0, 0))
    out = call(
        functools.partial(update_kernel, nm, nt),
        [(x.shape, x_spec)],
        [SMEM, x_spec, pl.BlockSpec((1, nb, nb), lambda l: (l, 0, 0)), ay_spec, ay_spec,
         proj_spec, proj_spec, whole(square), whole(wide), whole(wide), whole(wide), whole(square)],
        grid=(nl,),
        flops=12 * nl * nb**2 * nc,
        moved=12 << 20,
        scratch=[pltpu.VMEM((2 * nb, nc), jnp.bfloat16)] * 2,
    )(at, x, y_rows, half, other_half, half, other_half, mixer, y_cols, z_cols, v_cols, upper)[0]
    out = out.reshape(nl, nb, nt, nm, LANES).transpose(0, 1, 3, 2, 4)
    return out.reshape(hamiltonian.shape)


def solution(mesh):
    return jax.shard_map(
        body,
        mesh=mesh,
        in_specs=(P(None, "prow", None, "pcol"),),
        out_specs=P(None, "prow", None, "pcol"),
        check_vma=False,
    )
```

```python
import functools
import jax
import jax.numpy as jnp
from jax import lax
from jax.experimental import pallas as pl
from jax.experimental.pallas import tpu as pltpu
from jax.sharding import PartitionSpec as P

HP = lax.Precision.HIGHEST
XS, YS, CORES = 4, 4, 2
CHIPS = XS * YS
LANES = 128
BASE = 64
GROUP = 8
PLANE = [[q * CORES + k for q in range(CHIPS)] for k in range(CORES)]
LINE = YS * CORES
LINES = [[x * LINE + j for j in range(LINE)] for x in range(XS)]
SWAP = [(i, i ^ 1) for i in range(CHIPS * CORES)]
VMEM = pl.BlockSpec(memory_space=pltpu.VMEM)
SMEM = pl.BlockSpec(memory_space=pltpu.SMEM)


def mm(a, b):
    return jnp.dot(a, b, precision=HP, preferred_element_type=jnp.float32)


def mm_tn(a, b):
    return lax.dot_general(a, b, (((0,), (0,)), ((), ())), precision=HP, preferred_element_type=jnp.float32)


def mm_nt(a, b):
    return lax.dot_general(a, b, (((1,), (1,)), ((), ())), precision=HP, preferred_element_type=jnp.float32)


def eliminate(block, jordan):
    n = block.shape[0]
    eye = (lax.broadcasted_iota(jnp.int32, (n, n), 0) == lax.broadcasted_iota(jnp.int32, (n, n), 1))
    wide = jnp.concatenate([block, eye.astype(jnp.float32)], axis=1)
    shape = (GROUP, 2 * n)
    groups = n // GROUP
    at = lax.broadcasted_iota(jnp.int32, shape, 0)
    w = [wide[g * GROUP : (g + 1) * GROUP] for g in range(groups)]
    for p in range(groups):
        live = [g for g in range(groups) if jordan or g >= p]
        cols = {
            g: [
                jnp.broadcast_to(w[g][:, p * GROUP + b : p * GROUP + b + 1], shape)
                for b in range(GROUP)
            ]
            for g in live
        }
        for a in range(GROUP):
            inv = 1.0 / cols[p][a][a : a + 1]
            row = w[p][a : a + 1]
            heads = [cols[p][b][a : a + 1] for b in range(GROUP)]
            for g in live:
                m = cols[g][a] * inv
                if g == p:
                    m = jnp.where(at != a if jordan else at > a, m, 0.0)
                for b in range(a + 1, GROUP):
                    cols[g][b] = cols[g][b] - m * heads[b]
                w[g] = w[g] - m * row
    return jnp.concatenate(w, axis=0)


def diagonal(wide):
    n = wide.shape[0]
    shape = wide.shape
    eye = lax.broadcasted_iota(jnp.int32, shape, 0) == lax.broadcasted_iota(jnp.int32, shape, 1)
    return jnp.sum(jnp.where(eye, wide, 0.0), axis=1, keepdims=True)


def factor(a):
    n = a.shape[0]
    if n <= BASE:
        wide = eliminate(a, False)
        wide = wide * (1.0 / jnp.sqrt(diagonal(wide)))
        left = wide[:, :n]
        upper = lax.broadcasted_iota(jnp.int32, (n, n), 0) <= lax.broadcasted_iota(jnp.int32, (n, n), 1)
        return jnp.where(upper, left, 0.0), wide[:, n:]
    h = n // 2
    u11, i11 = factor(a[:h, :h])
    u12 = mm(i11, a[:h, h:])
    u22, i22 = factor(a[h:, h:] - mm_tn(u12, u12))
    i21 = -mm(i22, mm_tn(u12, i11))
    zero = jnp.zeros((h, h), jnp.float32)
    upper = jnp.concatenate([jnp.concatenate([u11, u12], 1), jnp.concatenate([zero, u22], 1)], 0)
    inv = jnp.concatenate([jnp.concatenate([i11, zero], 1), jnp.concatenate([i21, i22], 1)], 0)
    return upper, inv


def inverse(a):
    n = a.shape[0]
    if n <= BASE:
        wide = eliminate(a, True)
        return (wide * (1.0 / diagonal(wide)))[:, n:]
    h = n // 2
    i11 = inverse(a[:h, :h])
    x = mm(i11, a[:h, h:])
    y = mm(a[h:, :h], i11)
    s = inverse(a[h:, h:] - mm(a[h:, :h], x))
    xs = mm(x, s)
    top = jnp.concatenate([i11 + mm(xs, y), -xs], 1)
    return jnp.concatenate([top, jnp.concatenate([-mm(s, y), s], 1)], 0)


def split(a):
    high = a.astype(jnp.bfloat16)
    return high, (a - high.astype(jnp.float32)).astype(jnp.bfloat16)


def dot3(a, b, dims):
    one = functools.partial(
        lax.dot_general, dimension_numbers=(dims, ((), ())), preferred_element_type=jnp.float32
    )
    return one(a[0], b[0]) + (one(a[0], b[1]) + one(a[1], b[0]))


def identity(n):
    rows = lax.broadcasted_iota(jnp.int32, (n, n), 0)
    return (rows == lax.broadcasted_iota(jnp.int32, (n, n), 1)).astype(jnp.float32)


def tile(ref, m, t, nm, nt):
    return ref[pl.ds(t * nm + m, ref.shape[0] // (nm * nt), stride=nm * nt), :]


def in_order(at_ref, own, other):
    first = at_ref[2] == 0
    return jnp.concatenate([jnp.where(first, own, other), jnp.where(first, other, own)], axis=0)


def rows_of(ref):
    return ref[...].reshape(-1, ref.shape[-1])


def pack_kernel(nm, nt, at_ref, x_ref, packet_ref, gram_ref):
    step = pl.program_id(0)
    panel = jnp.concatenate([tile(x_ref, 0, t, nm, nt) for t in range(nt)], axis=1)
    panel = jnp.where((step == 0) & (at_ref[0] == 0), 0.0, panel)
    last = packet_ref.shape[2] - 1
    packet_ref[:, :, pl.ds(step, 1)] = panel.reshape(CORES, CHIPS, 1, *packet_ref.shape[3:])
    more = mm_tn(panel, panel)

    @pl.when(step == 0)
    def _():
        gram_ref[...] = more

    @pl.when(step > 0)
    def _():
        gram_ref[...] += more

    @pl.when(step == last - 1)
    def _():
        packet_ref[:, :, last] = gram_ref[...].reshape(CORES, CHIPS, *packet_ref.shape[3:])


def factor_kernel(at_ref, own_ref, other_ref, upper_ref, inv_ref, inv_t_ref):
    upper, inv = factor(in_order(at_ref, rows_of(own_ref), rows_of(other_ref)))
    upper_ref[...] = upper
    inv_ref[...] = inv
    inv_t_ref[...] = inv.T


def mixer_kernel(at_ref, own_ref, other_ref, inv_ref, after_ref, mixer_ref):
    top = in_order(at_ref, rows_of(own_ref), rows_of(other_ref))
    mixer_ref[...] = inverse(identity(top.shape[0]) + mm_nt(inv_ref[...], top))


def rows_kernel(at_ref, own_ref, other_ref, inv_t_ref, y_ref, slab_ref, flip_ref):
    y = mm(in_order(at_ref, rows_of(own_ref), rows_of(other_ref)), inv_t_ref[...])
    y += jnp.where((pl.program_id(0) == 0) & (at_ref[0] == 1), identity(y.shape[0]), 0.0)
    y_ref[0] = y
    flip_ref[...] = y.T
    deep = slab_ref.shape[0]
    slab_ref[...] = flip_ref[pl.ds(pl.multiple_of(at_ref[3] * deep, deep), deep), :]


def apply_kernel(
    nm, nt, at_ref, x_ref, top_ref, far_ref, more_ref, inv_ref, keep_ref, send_ref, y_ref, high_ref, low_ref
):
    step = pl.program_id(0)
    nb = inv_ref.shape[0]

    @pl.when(step == 0)
    def _():
        for m in range(nm):
            panel = jnp.concatenate(
                [
                    jnp.where(
                        at_ref[4] == 1,
                        tile(top_ref, m, t, nm, nt),
                        tile(far_ref, m, t, nm, nt) + tile(more_ref, m, t, nm, nt),
                    )
                    for t in range(nt)
                ],
                axis=1,
            )
            if m == 0:
                panel = jnp.where(at_ref[1] == 0, 0.0, panel)
            y = mm(inv_ref[...], panel)
            if m == 0:
                y += jnp.where(at_ref[1] == 1, identity(nb), 0.0)
            y_ref[:, m * nb : (m + 1) * nb] = y
            high_ref[m * nb : (m + 1) * nb], low_ref[m * nb : (m + 1) * nb] = split(y.T)

    block = jnp.concatenate(
        [tile(x_ref, m, t, nm, nt) for m in range(nm) for t in range(nt)], axis=1
    )
    part = dot3(split(block), (high_ref[...], low_ref[...]), ((1,), (0,)))
    part = jnp.where((step == 0) & (at_ref[0] == 0), 0.0, part)
    first = at_ref[2] == 0
    hb = nb // CORES
    keep_ref[...] = jnp.where(first, part[:hb], part[hb:]).reshape(keep_ref.shape)
    send_ref[...] = jnp.where(first, part[hb:], part[:hb]).reshape(send_ref.shape)


def proj_kernel(at_ref, slab_ref, own_ref, other_ref, copies_ref):
    step = pl.program_id(0)
    more = mm(slab_ref[...], in_order(at_ref, rows_of(own_ref), rows_of(other_ref)))

    @pl.when(step == 0)
    def _():
        copies_ref[0] = more

    @pl.when(step > 0)
    def _():
        copies_ref[0] += more

    @pl.when(step == pl.num_programs(0) - 1)
    def _():
        for i in range(1, copies_ref.shape[0]):
            copies_ref[i] = copies_ref[0]


def sides_kernel(at_ref, mixer_ref, y_ref, near_ref, far_ref, more_ref, z_ref, v_ref):
    mixer = mixer_ref[...]
    nb = mixer.shape[0]
    for m in range(y_ref.shape[1] // nb):
        halves = [
            jnp.where(at_ref[5] == 1, near_ref[h, :, m], far_ref[h, :, m] + more_ref[h, :, m])
            for h in range(CORES)
        ]
        ay = in_order(at_ref, *[half.reshape(nb // CORES, nb) for half in halves])
        z_ref[:, m * nb : (m + 1) * nb] = lax.dot_general(
            mixer, ay, (((0,), (1,)), ((), ())), precision=HP, preferred_element_type=jnp.float32
        )
    v_ref[...] = mm(mixer, y_ref[...])


def update_kernel(
    nm, nt, at_ref, x_ref, left_ref, own_ref, other_ref, proj_ref,
    mixer_ref, y_ref, z_ref, v_ref, upper_ref, out_ref, high_ref, low_ref,
):
    step = pl.program_id(0)
    nb = mixer_ref.shape[0]

    @pl.when(step == 0)
    def _():
        mixer = mixer_ref[...]
        core = mm(mm_tn(mixer, proj_ref[...]), mixer)
        w = split(z_ref[...] - mm_tn(core, y_ref[...]))
        v = split(v_ref[...])
        for i, ref in enumerate((high_ref, low_ref)):
            ref[:nb] = w[i]
            ref[nb:] = v[i]

    ay = in_order(at_ref, rows_of(own_ref), rows_of(other_ref))
    left = split(jnp.concatenate([left_ref[0], ay], axis=1))
    change = dot3(left, (high_ref[...], low_ref[...]), ((1,), (0,)))
    rows = nb
    for m in range(nm):
        for t in range(nt):
            at = m * nb + t * LANES
            out_ref[pl.ds(t * nm + m, rows, stride=nm * nt), :] = (
                tile(x_ref, m, t, nm, nt) - change[:, at : at + LANES]
            )

    @pl.when(at_ref[1] == 0)
    def _():
        keep = (step == 0) & (at_ref[0] == 0)
        band = jnp.where((step == 0) & (at_ref[0] == 1), -upper_ref[...], 0.0)
        for t in range(nt):
            old = tile(x_ref, 0, t, nm, nt)
            out_ref[pl.ds(t * nm, rows, stride=nm * nt), :] = jnp.where(
                keep, old, band[:, t * LANES : (t + 1) * LANES]
            )

    @pl.when((step == 0) & (at_ref[0] == 0))
    def _():
        band = jnp.where(at_ref[1] == 1, -upper_ref[...].T, 0.0)
        for m in range(nm):
            for t in range(nt):
                new = band[:, t * LANES : (t + 1) * LANES] if m == 0 else jnp.zeros((rows, LANES))
                if m == 0:
                    new = jnp.where(at_ref[1] == 0, tile(x_ref, m, t, nm, nt), new)
                out_ref[pl.ds(t * nm + m, rows, stride=nm * nt), :] = new


def call(kernel, outs, ins, grid=(), flops=0, moved=1 << 20, scratch=()):
    return pl.pallas_call(
        kernel,
        grid=grid,
        out_shape=[jax.ShapeDtypeStruct(s, jnp.float32) for s, _ in outs],
        in_specs=ins,
        out_specs=[spec for _, spec in outs],
        scratch_shapes=list(scratch),
        compiler_params=pltpu.CompilerParams(vmem_limit_bytes=40 << 20),
        cost_estimate=pl.CostEstimate(flops=flops, bytes_accessed=moved, transcendentals=0),
    )


def share(piece, axis, count, groups=None):
    copies = jnp.broadcast_to(piece[None], (count,) + piece.shape)
    return lax.all_to_all(copies, axis, 0, 0, axis_index_groups=groups)


def move(block, root, nz, hops):
    lines = CHIPS * CORES
    pairs = [
        ((root(c) + i) % nz * lines + c, (root(c) + j) % nz * lines + c)
        for c in range(lines)
        for i, j in hops
    ]
    return lax.ppermute(block, ("prow", "pcol"), pairs)


def near_moves(block, root, nz):
    return move(block, root, nz, [(0, 3)]), move(block, root, nz, [(0, 6)])


def far_moves(block, root, nz):
    return move(block, root, nz, [(0, 1), (3, 4)]), move(block, root, nz, [(0, 7), (3, 2), (6, 5)])


def body(hamiltonian):
    nl, nb, nm, _ = hamiltonian.shape
    nt = nb // LANES
    nz = lax.axis_size("prow")
    prow = lax.axis_index("prow")
    pcol = lax.axis_index("pcol")
    core = pcol % CORES
    sub = nb // (CHIPS * CORES)
    nc = nm * nb
    away = (prow + nz - pcol % nz) % nz
    relay = lambda d: (d == 0) | (d == 3) | (d == 6)
    at = jnp.stack([prow, pcol, core, pcol % LINE, relay(prow), relay(away)]).astype(jnp.int32)
    square, wide = (nb, nb), (nb, nc)
    whole = lambda shape: pl.BlockSpec(shape, lambda l: (0,) * len(shape))
    chunk = lambda index: pl.BlockSpec((CHIPS, 1, sub, nb), index)
    barrier = lax.optimization_barrier

    x = hamiltonian.reshape(nl, nb, nm, nt, LANES).transpose(0, 1, 3, 2, 4)
    x = x.reshape(nl * nb * nt * nm, LANES)
    x_rows = nb * nt * nm
    x_spec = pl.BlockSpec((x_rows, LANES), lambda l: (l, 0))

    root = lambda c: 0
    near = near_moves(x[:x_rows], root, nz)

    packet_shape = (CORES, CHIPS, nl + 1, sub, nb)
    packet = call(
        functools.partial(pack_kernel, nm, nt),
        [(packet_shape, whole(packet_shape))],
        [SMEM, x_spec],
        grid=(nl,),
        flops=2 * 10**10,
        moved=6 << 20,
        scratch=[pltpu.VMEM(square, jnp.float32)],
    )(at, x)[0]
    outgoing = jnp.where(core == 0, packet[0], lax.ppermute(packet[1], "pcol", [(0, 1)]))
    mine = lax.all_to_all(outgoing, "pcol", 0, 0, axis_index_groups=PLANE)[0]
    near, mine = barrier((near, mine))
    p_cols = jnp.where(prow == 0, x[:x_rows], near[0] + near[1])
    stacked = share(jnp.stack([mine[nl], mine[0]]), "prow", nz)
    summed = jnp.stack([jnp.sum(stacked[:, 0], axis=0), stacked[1, 1]])
    small = share(summed, "pcol", CHIPS, PLANE)
    p_cols, small, mine = barrier((p_cols, small, mine))
    far = far_moves(p_cols, root, nz)
    other_small = lax.ppermute(small, "pcol", SWAP)
    gram_spec = chunk(lambda l: (0, 0, 0, 0))
    upper, inv, inv_t = call(
        factor_kernel, [(square, VMEM)] * 3, [SMEM, gram_spec, gram_spec], grid=(1,), flops=10**10
    )(at, small, other_small)
    own_p = share(mine[:nl], "pcol", CHIPS, PLANE)
    far, inv, inv_t = barrier((far, inv, inv_t))

    half_shape = (CHIPS, nl, sub, nb)
    row_spec = chunk(lambda l: (0, l, 0, 0))
    keep, send, y_cols = call(
        functools.partial(apply_kernel, nm, nt),
        [(half_shape, row_spec), (half_shape, row_spec), (wide, whole(wide))],
        [SMEM, x_spec] + [whole((x_rows, LANES))] * 3 + [whole(square)],
        grid=(nl,),
        flops=12 * nl * nb**2 * nc,
        moved=9 << 20,
        scratch=[pltpu.VMEM((nc, nb), jnp.bfloat16)] * 2,
    )(at, x, p_cols, *far, inv)
    keep, send, own_p = barrier((keep, send, own_p))
    other_p = lax.ppermute(own_p, "pcol", SWAP)
    parts = keep + lax.ppermute(send, "pcol", SWAP)
    parts = lax.all_to_all(parts, "pcol", 0, 0, axis_index_groups=PLANE)
    slab_rows = nb // LINE
    y_rows, slab = call(
        rows_kernel,
        [((nl, nb, nb), pl.BlockSpec((1, nb, nb), lambda l: (l, 0, 0))),
         ((slab_rows, nl * nb), pl.BlockSpec((slab_rows, nb), lambda l: (0, l)))],
        [SMEM, row_spec, row_spec, whole(square)],
        grid=(nl,),
        flops=5 * 10**9,
        moved=6 << 20,
        scratch=[pltpu.VMEM(square, jnp.float32)],
    )(at, own_p, other_p, inv_t)
    parts, y_rows, slab = barrier((parts, y_rows, slab))
    own = share(jnp.sum(parts, axis=0), "pcol", CHIPS, PLANE)
    mixer = call(
        mixer_kernel,
        [(square, VMEM)],
        [SMEM] + [chunk(lambda l: (0, 1, 0, 0))] * 2 + [VMEM, pl.BlockSpec(memory_space=pl.ANY)],
        grid=(1,),
        flops=10**10,
    )(at, small, other_small, inv, parts)[0]
    own, mixer = barrier((own, mixer))
    other = lax.ppermute(own, "pcol", SWAP)

    picked = jnp.stack(
        [
            jnp.stack(
                [lax.dynamic_index_in_dim(a, m * XS + pcol // nz, 1, keepdims=False) for m in range(nm)], 1
            )
            for a in (own, other)
        ]
    )
    root = lambda c: c % nz
    near = near_moves(picked, root, nz)

    copies = call(
        proj_kernel,
        [((nz, slab_rows, nb), whole((nz, slab_rows, nb)))],
        [SMEM, pl.BlockSpec((slab_rows, nb), lambda l: (0, l)), row_spec, row_spec],
        grid=(nl,),
        flops=10**9,
        moved=4 << 20,
    )(at, slab, own, other)[0]
    pieces = lax.all_to_all(copies, "prow", 0, 0)
    near, pieces = barrier((near, pieces))
    ay_cols = jnp.where(away == 0, picked, near[0] + near[1])
    far = far_moves(ay_cols, root, nz)
    proj = share(jnp.sum(pieces, axis=0), "pcol", LINE, LINES).reshape(square)
    far, proj = barrier((far, proj))
    z_cols, v_cols = call(sides_kernel, [(wide, VMEM)] * 2, [SMEM] + [VMEM] * 5, flops=3 * 10**9)(
        at, mixer, y_cols, ay_cols, *far
    )

    out = call(
        functools.partial(update_kernel, nm, nt),
        [(x.shape, x_spec)],
        [SMEM, x_spec, pl.BlockSpec((1, nb, nb), lambda l: (l, 0, 0)), row_spec, row_spec]
        + [whole(s) for s in (square, square, wide, wide, wide, square)],
        grid=(nl,),
        flops=12 * nl * nb**2 * nc,
        moved=12 << 20,
        scratch=[pltpu.VMEM((2 * nb, nc), jnp.bfloat16)] * 2,
    )(at, x, y_rows, own, other, proj, mixer, y_cols, z_cols, v_cols, upper)[0]
    out = out.reshape(nl, nb, nt, nm, LANES).transpose(0, 1, 3, 2, 4)
    return out.reshape(hamiltonian.shape)


def solution(mesh):
    return jax.shard_map(
        body,
        mesh=mesh,
        in_specs=(P(None, "prow", None, "pcol"),),
        out_specs=P(None, "prow", None, "pcol"),
        check_vma=False,
    )
```

```python
import functools
import jax
import jax.numpy as jnp
from jax import lax
from jax.experimental import pallas as pl
from jax.experimental.pallas import tpu as pltpu
from jax.sharding import PartitionSpec as P

HP = lax.Precision.HIGHEST
XS, YS, CORES = 4, 4, 2
CHIPS = XS * YS
LANES = 128
BASE = 64
GROUP = 8
PLANE = [[q * CORES + k for q in range(CHIPS)] for k in range(CORES)]
SWAP = [(i, i ^ 1) for i in range(CHIPS * CORES)]
VMEM = pl.BlockSpec(memory_space=pltpu.VMEM)
SMEM = pl.BlockSpec(memory_space=pltpu.SMEM)
HBM = pl.BlockSpec(memory_space=pltpu.HBM)


def mm(a, b):
    return jnp.dot(a, b, precision=HP, preferred_element_type=jnp.float32)


def mm_tn(a, b):
    return lax.dot_general(a, b, (((0,), (0,)), ((), ())), precision=HP, preferred_element_type=jnp.float32)


def mm_nt(a, b):
    return lax.dot_general(a, b, (((1,), (1,)), ((), ())), precision=HP, preferred_element_type=jnp.float32)


def eliminate(block, jordan):
    n = block.shape[0]
    eye = (lax.broadcasted_iota(jnp.int32, (n, n), 0) == lax.broadcasted_iota(jnp.int32, (n, n), 1))
    wide = jnp.concatenate([block, eye.astype(jnp.float32)], axis=1)
    shape = (GROUP, 2 * n)
    groups = n // GROUP
    at = lax.broadcasted_iota(jnp.int32, shape, 0)
    w = [wide[g * GROUP : (g + 1) * GROUP] for g in range(groups)]
    for p in range(groups):
        live = [g for g in range(groups) if jordan or g >= p]
        cols = {
            g: [
                jnp.broadcast_to(w[g][:, p * GROUP + b : p * GROUP + b + 1], shape)
                for b in range(GROUP)
            ]
            for g in live
        }
        for a in range(GROUP):
            inv = 1.0 / cols[p][a][a : a + 1]
            row = w[p][a : a + 1]
            heads = [cols[p][b][a : a + 1] for b in range(GROUP)]
            for g in live:
                m = cols[g][a] * inv
                if g == p:
                    m = jnp.where(at != a if jordan else at > a, m, 0.0)
                for b in range(a + 1, GROUP):
                    cols[g][b] = cols[g][b] - m * heads[b]
                w[g] = w[g] - m * row
    return jnp.concatenate(w, axis=0)


def diagonal(wide):
    n = wide.shape[0]
    shape = wide.shape
    eye = lax.broadcasted_iota(jnp.int32, shape, 0) == lax.broadcasted_iota(jnp.int32, shape, 1)
    return jnp.sum(jnp.where(eye, wide, 0.0), axis=1, keepdims=True)


def factor(a):
    n = a.shape[0]
    if n <= BASE:
        wide = eliminate(a, False)
        wide = wide * (1.0 / jnp.sqrt(diagonal(wide)))
        left = wide[:, :n]
        upper = lax.broadcasted_iota(jnp.int32, (n, n), 0) <= lax.broadcasted_iota(jnp.int32, (n, n), 1)
        return jnp.where(upper, left, 0.0), wide[:, n:]
    h = n // 2
    u11, i11 = factor(a[:h, :h])
    u12 = mm(i11, a[:h, h:])
    u22, i22 = factor(a[h:, h:] - mm_tn(u12, u12))
    i21 = -mm(i22, mm_tn(u12, i11))
    zero = jnp.zeros((h, h), jnp.float32)
    upper = jnp.concatenate([jnp.concatenate([u11, u12], 1), jnp.concatenate([zero, u22], 1)], 0)
    inv = jnp.concatenate([jnp.concatenate([i11, zero], 1), jnp.concatenate([i21, i22], 1)], 0)
    return upper, inv


def inverse(a):
    n = a.shape[0]
    if n <= BASE:
        wide = eliminate(a, True)
        return (wide * (1.0 / diagonal(wide)))[:, n:]
    h = n // 2
    i11 = inverse(a[:h, :h])
    x = mm(i11, a[:h, h:])
    y = mm(a[h:, :h], i11)
    s = inverse(a[h:, h:] - mm(a[h:, :h], x))
    xs = mm(x, s)
    top = jnp.concatenate([i11 + mm(xs, y), -xs], 1)
    return jnp.concatenate([top, jnp.concatenate([-mm(s, y), s], 1)], 0)


def halves(a):
    high = a.astype(jnp.bfloat16)
    return high, (a - high.astype(jnp.float32)).astype(jnp.bfloat16)


def thrice(a, left):
    high, low = halves(a)
    return jnp.concatenate([high, low, high] if left else [high, high, low], axis=1 if left else 0)


def mm3(left, right):
    return jnp.dot(left, right, preferred_element_type=jnp.float32)


def identity(n):
    rows = lax.broadcasted_iota(jnp.int32, (n, n), 0)
    return (rows == lax.broadcasted_iota(jnp.int32, (n, n), 1)).astype(jnp.float32)


def tile(ref, m, t, nm, nt):
    return ref[pl.ds(t * nm + m, ref.shape[0] // (nm * nt), stride=nm * nt), :]


def fetched(step, x_ref, held_ref, sems):
    rows = held_ref.shape[1]
    copy = lambda i: pltpu.make_async_copy(
        x_ref.at[pl.ds(pl.multiple_of(i * rows, rows), rows)], held_ref.at[i], sems.at[i]
    )

    @pl.when(step == 0)
    def _():
        for i in range(held_ref.shape[0]):
            copy(i).start()

    copy(step).wait()
    return held_ref.at[step]


def in_order(at_ref, own, other):
    first = at_ref[2] == 0
    return jnp.concatenate([jnp.where(first, own, other), jnp.where(first, other, own)], axis=0)


def rows_of(ref):
    return ref[...].reshape(-1, ref.shape[-1])


def pack_kernel(nm, nt, at_ref, x_ref, packet_ref, gram_ref, held_ref, sems):
    step = pl.program_id(0)
    x_ref = fetched(step, x_ref, held_ref, sems)
    panel = jnp.concatenate([tile(x_ref, 0, t, nm, nt) for t in range(nt)], axis=1)
    panel = jnp.where((step == 0) & (at_ref[0] == 0), 0.0, panel)
    last = packet_ref.shape[2] - 1
    packet_ref[:, :, pl.ds(step, 1)] = panel.reshape(CORES, CHIPS, 1, *packet_ref.shape[3:])
    more = mm_tn(panel, panel)

    @pl.when(step == 0)
    def _():
        gram_ref[...] = more

    @pl.when(step > 0)
    def _():
        gram_ref[...] += more

    @pl.when(step == last - 1)
    def _():
        packet_ref[:, :, last] = gram_ref[...].reshape(CORES, CHIPS, *packet_ref.shape[3:])


def factor_kernel(at_ref, own_ref, other_ref, upper_ref, inv_ref, inv_t_ref):
    upper, inv = factor(in_order(at_ref, rows_of(own_ref), rows_of(other_ref)))
    upper_ref[...] = upper
    inv_ref[...] = inv
    inv_t_ref[...] = inv.T


def mixer_kernel(at_ref, own_ref, other_ref, inv_ref, after_ref, mixer_ref):
    top = in_order(at_ref, rows_of(own_ref), rows_of(other_ref))
    mixer_ref[...] = inverse(identity(top.shape[0]) + mm_nt(inv_ref[...], top))


def rows_kernel(at_ref, own_ref, other_ref, inv_t_ref, y_ref, slab_ref, flip_ref):
    y = mm(in_order(at_ref, rows_of(own_ref), rows_of(other_ref)), inv_t_ref[...])
    y += jnp.where((pl.program_id(0) == 0) & (at_ref[0] == 1), identity(y.shape[0]), 0.0)
    y_ref[0] = y
    flip_ref[...] = y.T
    deep = slab_ref.shape[0]
    slab_ref[...] = flip_ref[pl.ds(pl.multiple_of(at_ref[3] * deep, deep), deep), :]


def apply_kernel(
    nm, nt, at_ref, x_ref, top_ref, far_ref, more_ref, inv_ref, keep_ref, send_ref, y_ref,
    right_ref,
):
    step = pl.program_id(0)
    nb = inv_ref.shape[0]

    @pl.when(step == 0)
    def _():
        for m in range(nm):
            panel = jnp.concatenate(
                [
                    jnp.where(
                        at_ref[4] == 1,
                        tile(top_ref, m, t, nm, nt),
                        tile(far_ref, m, t, nm, nt) + tile(more_ref, m, t, nm, nt),
                    )
                    for t in range(nt)
                ],
                axis=1,
            )
            if m == 0:
                panel = jnp.where(at_ref[1] == 0, 0.0, panel)
            y = mm(inv_ref[...], panel)
            if m == 0:
                y += jnp.where(at_ref[1] == 1, identity(nb), 0.0)
            y_ref[:, m * nb : (m + 1) * nb] = y
        right_ref[...] = thrice(y_ref[...].T, False)

    block = jnp.concatenate(
        [tile(x_ref, m, t, nm, nt) for m in range(nm) for t in range(nt)], axis=1
    )
    part = mm3(thrice(block, True), right_ref[...])
    part = jnp.where((step == 0) & (at_ref[0] == 0), 0.0, part)
    first = at_ref[2] == 0
    hb = nb // CORES
    keep_ref[0] = jnp.where(first, part[:hb], part[hb:])
    send_ref[0] = jnp.where(first, part[hb:], part[:hb])


def proj_kernel(at_ref, slab_ref, own_ref, other_ref, copies_ref):
    step = pl.program_id(0)
    more = mm(slab_ref[...], in_order(at_ref, rows_of(own_ref), rows_of(other_ref)))

    @pl.when(step == 0)
    def _():
        copies_ref[0] = more

    @pl.when(step > 0)
    def _():
        copies_ref[0] += more

    @pl.when(step == pl.num_programs(0) - 1)
    def _():
        for i in range(1, copies_ref.shape[0]):
            copies_ref[i] = copies_ref[0]


def route_kernel(nm, at_ref, four_ref, more_ref, pieces_ref, out_ref):
    nz, sub, nb = pieces_ref.shape
    total = jnp.sum(pieces_ref[...], axis=0)
    deep = four_ref.shape[1] // nm
    for z in range(nz):
        bits = z ^ at_ref[0]
        place = (bits & 2) | ((bits >> 2) & 1)

        def put(ref):
            for m in range(nm):
                for i in range(deep):
                    out_ref[i * nz + z, m] = ref[place, m * deep + i]

        @pl.when((bits & 1) == 0)
        def _():
            put(four_ref)

        @pl.when((bits & 1) == 1)
        def _():
            put(more_ref)

    for i in range(out_ref.shape[0]):
        out_ref[i, nm] = total


def sides_kernel(mixer_ref, y_ref, rows_ref, z_ref, v_ref, proj_ref):
    mixer = mixer_ref[...]
    nb = mixer.shape[0]
    nm = y_ref.shape[1] // nb

    def gathered(m):
        return jnp.concatenate(
            [rows_ref[:, k, m].reshape(nb // CORES, nb) for k in range(CORES)], axis=0
        )

    for m in range(nm):
        z_ref[:, m * nb : (m + 1) * nb] = lax.dot_general(
            mixer, gathered(m), (((0,), (1,)), ((), ())), precision=HP, preferred_element_type=jnp.float32
        )
    v_ref[...] = mm(mixer, y_ref[...])
    proj_ref[...] = gathered(nm)


def update_kernel(
    nm, nt, at_ref, x_ref, left_ref, own_ref, other_ref, proj_ref,
    mixer_ref, y_ref, z_ref, v_ref, upper_ref, out_ref, right_ref,
):
    step = pl.program_id(0)
    nb = mixer_ref.shape[0]

    @pl.when(step == 0)
    def _():
        mixer = mixer_ref[...]
        core = mm(mm_tn(mixer, proj_ref[...]), mixer)
        w = z_ref[...] - mm_tn(core, y_ref[...])
        right_ref[...] = thrice(jnp.concatenate([w, v_ref[...]], axis=0), False)

    ay = in_order(at_ref, rows_of(own_ref), rows_of(other_ref))
    change = mm3(thrice(jnp.concatenate([left_ref[0], ay], axis=1), True), right_ref[...])
    rows = nb
    for m in range(nm):
        for t in range(nt):
            at = m * nb + t * LANES
            out_ref[pl.ds(t * nm + m, rows, stride=nm * nt), :] = (
                tile(x_ref, m, t, nm, nt) - change[:, at : at + LANES]
            )

    @pl.when(at_ref[1] == 0)
    def _():
        keep = (step == 0) & (at_ref[0] == 0)
        band = jnp.where((step == 0) & (at_ref[0] == 1), -upper_ref[...], 0.0)
        for t in range(nt):
            old = tile(x_ref, 0, t, nm, nt)
            out_ref[pl.ds(t * nm, rows, stride=nm * nt), :] = jnp.where(
                keep, old, band[:, t * LANES : (t + 1) * LANES]
            )

    @pl.when((step == 0) & (at_ref[0] == 0))
    def _():
        band = jnp.where(at_ref[1] == 1, -upper_ref[...].T, 0.0)
        for m in range(nm):
            for t in range(nt):
                new = band[:, t * LANES : (t + 1) * LANES] if m == 0 else jnp.zeros((rows, LANES))
                if m == 0:
                    new = jnp.where(at_ref[1] == 0, tile(x_ref, m, t, nm, nt), new)
                out_ref[pl.ds(t * nm + m, rows, stride=nm * nt), :] = new


def call(kernel, outs, ins, grid=(), flops=0, moved=1 << 20, scratch=(), out=jax.ShapeDtypeStruct):
    return pl.pallas_call(
        kernel,
        grid=grid,
        out_shape=[out(s, jnp.float32) for s, _ in outs],
        in_specs=ins,
        out_specs=[spec for _, spec in outs],
        scratch_shapes=list(scratch),
        compiler_params=pltpu.CompilerParams(vmem_limit_bytes=40 << 20),
        cost_estimate=pl.CostEstimate(flops=flops, bytes_accessed=moved, transcendentals=0),
    )


def share(piece, axis, count, groups=None):
    copies = jnp.broadcast_to(piece[None], (count,) + piece.shape)
    return lax.all_to_all(copies, axis, 0, 0, axis_index_groups=groups)


def move(block, hops):
    return lax.ppermute(block, "prow", hops)


def near_moves(block):
    return move(block, [(0, 3)]), move(block, [(0, 6)])


def far_moves(block):
    return move(block, [(0, 1), (3, 4)]), move(block, [(0, 7), (3, 2), (6, 5)])


def doubled(block, reach, nz):
    return jnp.concatenate([block, move(block, [(i, i ^ reach) for i in range(nz)])])


def body(hamiltonian):
    nl, nb, nm, _ = hamiltonian.shape
    nt = nb // LANES
    nz = lax.axis_size("prow")
    prow = lax.axis_index("prow")
    pcol = lax.axis_index("pcol")
    core = pcol % CORES
    sub = nb // (CHIPS * CORES)
    nc = nm * nb
    relay = (prow == 0) | (prow == 3) | (prow == 6)
    at = jnp.stack([prow, pcol, core, core * CHIPS + pcol // CORES, relay]).astype(jnp.int32)
    square, wide = (nb, nb), (nb, nc)
    whole = lambda shape: pl.BlockSpec(shape, lambda l: (0,) * len(shape))
    chunk = lambda index: pl.BlockSpec((CHIPS, 1, sub, nb), index)
    barrier = lax.optimization_barrier

    x = hamiltonian.reshape(nl, nb, nm, nt, LANES).transpose(0, 1, 3, 2, 4)
    x = x.reshape(nl * nb * nt * nm, LANES)
    x_rows = nb * nt * nm
    x_spec = pl.BlockSpec((x_rows, LANES), lambda l: (l, 0))

    first_rows = x[:x_rows]

    packet_shape = (CORES, CHIPS, nl + 1, sub, nb)
    packet = call(
        functools.partial(pack_kernel, nm, nt),
        [(packet_shape, whole(packet_shape))],
        [SMEM, HBM],
        grid=(nl,),
        flops=2 * 10**10,
        moved=6 << 20,
        scratch=[
            pltpu.VMEM(square, jnp.float32),
            pltpu.VMEM((nl, x_rows, LANES), jnp.float32),
            pltpu.SemaphoreType.DMA((nl,)),
        ],
    )(at, pltpu.with_memory_space_constraint(x, pltpu.HBM))[0]
    outgoing = jnp.where(core == 0, packet[0], lax.ppermute(packet[1], "pcol", [(0, 1)]))
    near = near_moves(first_rows)
    mine = lax.all_to_all(outgoing, "pcol", 0, 0, axis_index_groups=PLANE)[0]
    near, mine = barrier((near, mine))
    p_cols = jnp.where(prow == 0, first_rows, near[0] + near[1])
    stacked = share(jnp.stack([mine[nl], mine[0]]), "prow", nz)
    summed = jnp.stack([jnp.sum(stacked[:, 0], axis=0), stacked[1, 1]])
    small = share(summed, "pcol", CHIPS, PLANE)
    p_cols, small, mine = barrier((p_cols, small, mine))
    far = far_moves(p_cols)
    other_small = lax.ppermute(small, "pcol", SWAP)
    gram_spec = chunk(lambda l: (0, 0, 0, 0))
    upper, inv, inv_t = call(
        factor_kernel, [(square, VMEM)] * 3, [SMEM, gram_spec, gram_spec], grid=(1,), flops=10**10
    )(at, small, other_small)
    own_p = share(mine[:nl], "pcol", CHIPS, PLANE)

    half_shape = (nl, nb // CORES, nb)
    half_spec = pl.BlockSpec((1,) + half_shape[1:], lambda l: (l, 0, 0))
    row_spec = chunk(lambda l: (0, l, 0, 0))
    keep, send, y_cols = call(
        functools.partial(apply_kernel, nm, nt),
        [(half_shape, half_spec), (half_shape, half_spec), (wide, whole(wide))],
        [SMEM, x_spec] + [whole((x_rows, LANES))] * 3 + [whole(square)],
        grid=(nl,),
        flops=12 * nl * nb**2 * nc,
        moved=9 << 20,
        scratch=[pltpu.VMEM((3 * nc, nb), jnp.bfloat16)],
        out=pltpu.HBM,
    )(at, x, *[pltpu.with_memory_space_constraint(a, pltpu.HBM) for a in (p_cols, *far)], inv)
    keep, send, own_p = barrier((keep, send, own_p))
    other_p = lax.ppermute(own_p, "pcol", SWAP)
    parts = (keep + lax.ppermute(send, "pcol", SWAP)).reshape(nl, CHIPS, sub, nb).transpose(1, 0, 2, 3)
    parts = lax.all_to_all(parts, "pcol", 0, 0, axis_index_groups=PLANE)
    y_rows, slab = call(
        rows_kernel,
        [((nl, nb, nb), pl.BlockSpec((1, nb, nb), lambda l: (l, 0, 0))),
         ((sub, nl * nb), pl.BlockSpec((sub, nb), lambda l: (0, l)))],
        [SMEM, row_spec, row_spec, whole(square)],
        grid=(nl,),
        flops=5 * 10**9,
        moved=6 << 20,
        scratch=[pltpu.VMEM(square, jnp.float32)],
    )(at, own_p, other_p, inv_t)
    parts, y_rows, slab = barrier((parts, y_rows, slab))
    piece = jnp.sum(parts, axis=0)
    own = share(piece, "pcol", CHIPS, PLANE)
    mixer = call(
        mixer_kernel,
        [(square, VMEM)],
        [SMEM] + [chunk(lambda l: (0, 1, 0, 0))] * 2 + [VMEM, pl.BlockSpec(memory_space=pl.ANY)],
        grid=(1,),
        flops=10**10,
    )(at, small, other_small, inv, parts)[0]
    four = doubled(doubled(piece[None], 4, nz), 2, nz)
    own, mixer, four = barrier((own, mixer, four))
    other = lax.ppermute(own, "pcol", SWAP)

    copies = call(
        proj_kernel,
        [((nz, sub, nb), whole((nz, sub, nb)))],
        [SMEM, pl.BlockSpec((sub, nb), lambda l: (0, l)), row_spec, row_spec],
        grid=(nl,),
        flops=10**9,
        moved=4 << 20,
    )(at, slab, own, other)[0]
    pieces = lax.all_to_all(copies, "prow", 0, 0)
    more = move(four, [(i, i ^ 1) for i in range(nz)])
    more, pieces = barrier((more, pieces))
    lines = CHIPS * CORES
    routed = call(
        functools.partial(route_kernel, nm),
        [((lines, nm + 1, sub, nb), VMEM)],
        [SMEM] + [VMEM] * 3,
        flops=10**8,
    )(at, four, more, pieces)[0]
    routed = lax.all_to_all(routed, "pcol", 0, 0)
    z_cols, v_cols, proj = call(
        sides_kernel, [(wide, VMEM), (wide, VMEM), (square, VMEM)], [VMEM] * 3, flops=3 * 10**9
    )(mixer, y_cols, routed.reshape(CHIPS, CORES, nm + 1, sub, nb))

    out = call(
        functools.partial(update_kernel, nm, nt),
        [(x.shape, x_spec)],
        [SMEM, x_spec, pl.BlockSpec((1, nb, nb), lambda l: (l, 0, 0)), row_spec, row_spec]
        + [whole(s) for s in (square, square, wide, wide, wide, square)],
        grid=(nl,),
        flops=12 * nl * nb**2 * nc,
        moved=12 << 20,
        scratch=[pltpu.VMEM((6 * nb, nc), jnp.bfloat16)],
    )(at, x, y_rows, own, other, proj, mixer, y_cols, z_cols, v_cols, upper)[0]
    out = out.reshape(nl, nb, nt, nm, LANES).transpose(0, 1, 3, 2, 4)
    return out.reshape(hamiltonian.shape)


def solution(mesh):
    return jax.shard_map(
        body,
        mesh=mesh,
        in_specs=(P(None, "prow", None, "pcol"),),
        out_specs=P(None, "prow", None, "pcol"),
        check_vma=False,
    )
```

```python
import functools
import jax
import jax.numpy as jnp
from jax import lax
from jax.experimental import pallas as pl
from jax.experimental.pallas import tpu as pltpu
from jax.sharding import PartitionSpec as P

HP = lax.Precision.HIGHEST
XS, YS, CORES = 4, 4, 2
CHIPS = XS * YS
LANES = 128
BASE = 64
GROUP = 8
PLANE = [[q * CORES + k for q in range(CHIPS)] for k in range(CORES)]
SWAP = [(i, i ^ 1) for i in range(CHIPS * CORES)]
VMEM = pl.BlockSpec(memory_space=pltpu.VMEM)
SMEM = pl.BlockSpec(memory_space=pltpu.SMEM)
HBM = pl.BlockSpec(memory_space=pltpu.HBM)


def mm(a, b):
    return jnp.dot(a, b, precision=HP, preferred_element_type=jnp.float32)


def mm_tn(a, b):
    return lax.dot_general(a, b, (((0,), (0,)), ((), ())), precision=HP, preferred_element_type=jnp.float32)


def mm_nt(a, b):
    return lax.dot_general(a, b, (((1,), (1,)), ((), ())), precision=HP, preferred_element_type=jnp.float32)


def eliminate(block, jordan):
    n = block.shape[0]
    eye = (lax.broadcasted_iota(jnp.int32, (n, n), 0) == lax.broadcasted_iota(jnp.int32, (n, n), 1))
    wide = jnp.concatenate([block, eye.astype(jnp.float32)], axis=1)
    shape = (GROUP, 2 * n)
    groups = n // GROUP
    at = lax.broadcasted_iota(jnp.int32, shape, 0)
    w = [wide[g * GROUP : (g + 1) * GROUP] for g in range(groups)]
    for p in range(groups):
        live = [g for g in range(groups) if jordan or g >= p]
        cols = {
            g: [
                jnp.broadcast_to(w[g][:, p * GROUP + b : p * GROUP + b + 1], shape)
                for b in range(GROUP)
            ]
            for g in live
        }
        for a in range(GROUP):
            inv = 1.0 / cols[p][a][a : a + 1]
            row = w[p][a : a + 1]
            heads = [cols[p][b][a : a + 1] for b in range(GROUP)]
            for g in live:
                m = cols[g][a] * inv
                if g == p:
                    m = jnp.where(at != a if jordan else at > a, m, 0.0)
                for b in range(a + 1, GROUP):
                    cols[g][b] = cols[g][b] - m * heads[b]
                w[g] = w[g] - m * row
    return jnp.concatenate(w, axis=0)


def diagonal(wide):
    n = wide.shape[0]
    shape = wide.shape
    eye = lax.broadcasted_iota(jnp.int32, shape, 0) == lax.broadcasted_iota(jnp.int32, shape, 1)
    return jnp.sum(jnp.where(eye, wide, 0.0), axis=1, keepdims=True)


def factor(a):
    n = a.shape[0]
    if n <= BASE:
        wide = eliminate(a, False)
        wide = wide * (1.0 / jnp.sqrt(diagonal(wide)))
        left = wide[:, :n]
        upper = lax.broadcasted_iota(jnp.int32, (n, n), 0) <= lax.broadcasted_iota(jnp.int32, (n, n), 1)
        return jnp.where(upper, left, 0.0), wide[:, n:]
    h = n // 2
    u11, i11 = factor(a[:h, :h])
    u12 = mm(i11, a[:h, h:])
    u22, i22 = factor(a[h:, h:] - mm_tn(u12, u12))
    i21 = -mm(i22, mm_tn(u12, i11))
    zero = jnp.zeros((h, h), jnp.float32)
    upper = jnp.concatenate([jnp.concatenate([u11, u12], 1), jnp.concatenate([zero, u22], 1)], 0)
    inv = jnp.concatenate([jnp.concatenate([i11, zero], 1), jnp.concatenate([i21, i22], 1)], 0)
    return upper, inv


def inverse(a):
    n = a.shape[0]
    if n <= BASE:
        wide = eliminate(a, True)
        return (wide * (1.0 / diagonal(wide)))[:, n:]
    h = n // 2
    i11 = inverse(a[:h, :h])
    x = mm(i11, a[:h, h:])
    y = mm(a[h:, :h], i11)
    s = inverse(a[h:, h:] - mm(a[h:, :h], x))
    xs = mm(x, s)
    top = jnp.concatenate([i11 + mm(xs, y), -xs], 1)
    return jnp.concatenate([top, jnp.concatenate([-mm(s, y), s], 1)], 0)


def halves(a):
    high = a.astype(jnp.bfloat16)
    return high, (a - high.astype(jnp.float32)).astype(jnp.bfloat16)


def thrice(a, left):
    high, low = halves(a)
    return jnp.concatenate([high, low, high] if left else [high, high, low], axis=1 if left else 0)


def mm3(left, right):
    return jnp.dot(left, right, preferred_element_type=jnp.float32)


def identity(n):
    rows = lax.broadcasted_iota(jnp.int32, (n, n), 0)
    return (rows == lax.broadcasted_iota(jnp.int32, (n, n), 1)).astype(jnp.float32)


def tile(ref, m, t, nm, nt):
    return ref[pl.ds(t * nm + m, ref.shape[0] // (nm * nt), stride=nm * nt), :]


def fetched(step, x_ref, held_ref, sems):
    rows = held_ref.shape[1]
    copy = lambda i: pltpu.make_async_copy(
        x_ref.at[pl.ds(pl.multiple_of(i * rows, rows), rows)], held_ref.at[i], sems.at[i]
    )

    @pl.when(step == 0)
    def _():
        for i in range(held_ref.shape[0]):
            copy(i).start()

    copy(step).wait()
    return held_ref.at[step]


def in_order(at_ref, own, other):
    first = at_ref[2] == 0
    return jnp.concatenate([jnp.where(first, own, other), jnp.where(first, other, own)], axis=0)


def rows_of(ref):
    return ref[...].reshape(-1, ref.shape[-1])


def pack_kernel(nm, nt, at_ref, x_ref, packet_ref, gram_ref, held_ref, sems):
    step = pl.program_id(0)
    x_ref = fetched(step, x_ref, held_ref, sems)
    panel = jnp.concatenate([tile(x_ref, 0, t, nm, nt) for t in range(nt)], axis=1)
    panel = jnp.where((step == 0) & (at_ref[0] == 0), 0.0, panel)
    last = packet_ref.shape[2] - 1
    packet_ref[:, :, pl.ds(step, 1)] = panel.reshape(CORES, CHIPS, 1, *packet_ref.shape[3:])
    more = mm_tn(panel, panel)

    @pl.when(step == 0)
    def _():
        gram_ref[...] = more

    @pl.when(step > 0)
    def _():
        gram_ref[...] += more

    @pl.when(step == last - 1)
    def _():
        packet_ref[:, :, last] = gram_ref[...].reshape(CORES, CHIPS, *packet_ref.shape[3:])


def factor_kernel(
    at_ref, own_ref, other_ref, inv_ref, upper_hbm, inv_hbm, inv_t_hbm, upper_ref, inv_t_ref, sems
):
    upper, inv = factor(in_order(at_ref, rows_of(own_ref), rows_of(other_ref)))
    upper_ref[...] = upper
    inv_ref[...] = inv
    inv_t_ref[...] = inv.T
    stores = [
        pltpu.make_async_copy(src, dst, sems.at[i])
        for i, (src, dst) in enumerate(
            ((upper_ref, upper_hbm), (inv_ref, inv_hbm), (inv_t_ref, inv_t_hbm))
        )
    ]
    for store in stores:
        store.start()
    for store in stores:
        store.wait()


def mixer_kernel(at_ref, own_ref, other_ref, inv_ref, after_ref, mixer_ref):
    top = in_order(at_ref, rows_of(own_ref), rows_of(other_ref))
    mixer_ref[...] = inverse(identity(top.shape[0]) + mm_nt(inv_ref[...], top))


def rows_kernel(at_ref, own_ref, other_ref, inv_t_ref, y_ref, slab_ref, flip_ref):
    y = mm(in_order(at_ref, rows_of(own_ref), rows_of(other_ref)), inv_t_ref[...])
    y += jnp.where((pl.program_id(0) == 0) & (at_ref[0] == 1), identity(y.shape[0]), 0.0)
    y_ref[0] = y
    flip_ref[...] = y.T
    deep = slab_ref.shape[0]
    slab_ref[...] = flip_ref[pl.ds(pl.multiple_of(at_ref[3] * deep, deep), deep), :]


def apply_kernel(
    nm, nt, at_ref, x_ref, top_hbm, far_hbm, more_hbm, inv_ref, keep_ref, send_hbm, y_hbm,
    top_ref, far_ref, more_ref, y_ref, send_ref, in_sems, out_sem, send_sems,
):
    nl, hb, nb = keep_ref.shape
    rows = nb * nt * nm
    loads = [
        pltpu.make_async_copy(src, dst, in_sems.at[i])
        for i, (src, dst) in enumerate(
            ((top_hbm, top_ref), (far_hbm, far_ref), (more_hbm, more_ref))
        )
    ]
    for load in loads:
        load.start()
    for load in loads:
        load.wait()
    for m in range(nm):
        panel = jnp.concatenate(
            [
                jnp.where(
                    at_ref[4] == 1,
                    tile(top_ref, m, t, nm, nt),
                    tile(far_ref, m, t, nm, nt) + tile(more_ref, m, t, nm, nt),
                )
                for t in range(nt)
            ],
            axis=1,
        )
        if m == 0:
            panel = jnp.where(at_ref[1] == 0, 0.0, panel)
        y = mm(inv_ref[...], panel)
        if m == 0:
            y += jnp.where(at_ref[1] == 1, identity(nb), 0.0)
        y_ref[:, m * nb : (m + 1) * nb] = y
    store = pltpu.make_async_copy(y_ref, y_hbm, out_sem)
    store.start()
    right = thrice(y_ref[...].T, False)
    first = at_ref[2] == 0
    send = lambda step: pltpu.make_async_copy(send_ref.at[step], send_hbm.at[step], send_sems.at[step])

    @pl.loop(0, nl // 2)
    def _(pair):
        blocks = []
        for i in range(2):
            step = pair * 2 + i
            rows_ref = x_ref.at[pl.ds(pl.multiple_of(step * rows, rows), rows)]
            blocks.append(
                jnp.concatenate(
                    [tile(rows_ref, m, t, nm, nt) for m in range(nm) for t in range(nt)], axis=1
                )
            )
        both = mm3(thrice(jnp.concatenate(blocks, axis=0), True), right)
        for i in range(2):
            step = pair * 2 + i
            part = both[i * nb : (i + 1) * nb]
            if i == 0:
                part = jnp.where((pair == 0) & (at_ref[0] == 0), 0.0, part)
            keep_ref[step] = jnp.where(first, part[:hb], part[hb:])
            send_ref[step] = jnp.where(first, part[hb:], part[:hb])
            send(step).start()

    for step in range(nl):
        send(step).wait()
    store.wait()


def half_loads(pair, own_hbm, other_hbm, own_ref, other_ref, own_sems, other_sems):
    two = pl.ds(pair * 2, 2)
    return (
        pltpu.make_async_copy(own_hbm.at[:, two], own_ref.at[:, two], own_sems.at[pair]),
        pltpu.make_async_copy(other_hbm.at[:, two], other_ref.at[:, two], other_sems.at[pair]),
    )


def proj_kernel(
    at_ref, slab_ref, own_hbm, other_hbm, copies_ref, own_ref, other_ref, own_sems, other_sems
):
    nl = own_ref.shape[1]
    nb = own_ref.shape[3]
    loads = [
        half_loads(p, own_hbm, other_hbm, own_ref, other_ref, own_sems, other_sems)
        for p in range(nl // 2)
    ]
    for pair in loads:
        for load in pair:
            load.start()
    total = jnp.zeros(copies_ref.shape[1:], jnp.float32)
    for step in range(nl):
        if step % 2 == 0:
            for load in loads[step // 2]:
                load.wait()
        ay = in_order(
            at_ref, *[ref[:, step].reshape(nb // CORES, nb) for ref in (own_ref, other_ref)]
        )
        total += mm(slab_ref[:, step * nb : (step + 1) * nb], ay)
    for i in range(copies_ref.shape[0]):
        copies_ref[i] = total


def route_kernel(nm, at_ref, four_ref, more_ref, pieces_ref, out_ref):
    nz, sub, nb = pieces_ref.shape
    total = jnp.sum(pieces_ref[...], axis=0)
    deep = four_ref.shape[1] // nm
    for z in range(nz):
        bits = z ^ at_ref[0]
        place = (bits & 2) | ((bits >> 2) & 1)

        def put(ref):
            for m in range(nm):
                for i in range(deep):
                    out_ref[i * nz + z, m] = ref[place, m * deep + i]

        @pl.when((bits & 1) == 0)
        def _():
            put(four_ref)

        @pl.when((bits & 1) == 1)
        def _():
            put(more_ref)

    for i in range(out_ref.shape[0]):
        out_ref[i, nm] = total


def update_kernel(
    nm, nt, at_ref, x_hbm, left_hbm, own_hbm, other_hbm, rows_ref, mixer_ref, y_hbm, upper_hbm,
    out_ref, right_ref, held_ref, y_ref, upper_ref, x_ref, left_ref, own_ref, other_ref,
    sems, in_sems, x_sems, left_sems, own_sems, other_sems,
):
    nb = mixer_ref.shape[0]
    nl = left_ref.shape[0]
    rows = nb * nt * nm

    def pair_loads(pair):
        at = pl.ds(pl.multiple_of(pair * 2 * rows, 2 * rows), 2 * rows)
        two = pl.ds(pair * 2, 2)
        return (
            pltpu.make_async_copy(x_hbm.at[at], x_ref.at[at], x_sems.at[pair]),
            pltpu.make_async_copy(left_hbm.at[two], left_ref.at[two], left_sems.at[pair]),
        ) + half_loads(pair, own_hbm, other_hbm, own_ref, other_ref, own_sems, other_sems)

    loads = [
        pltpu.make_async_copy(src, dst, in_sems.at[i])
        for i, (src, dst) in enumerate(((y_hbm, y_ref), (upper_hbm, upper_ref)))
    ]
    for load in loads:
        load.start()
    for pair in range(nl // 2):
        for load in pair_loads(pair):
            load.start()
    mixer = mixer_ref[...]

    def gathered(m):
        return jnp.concatenate(
            [rows_ref[:, k, m].reshape(nb // CORES, nb) for k in range(CORES)], axis=0
        )

    core = mm(mm_tn(mixer, gathered(nm)), mixer)
    z = lax.dot_general(
        mixer,
        jnp.concatenate([gathered(m) for m in range(nm)], axis=0),
        (((0,), (1,)), ((), ())),
        precision=HP,
        preferred_element_type=jnp.float32,
    )
    for load in loads:
        load.wait()
    y = y_ref[...]
    right_ref[...] = thrice(jnp.concatenate([z - mm_tn(core, y), mm(mixer, y)], axis=0), False)

    def copy(pair):
        return pltpu.make_async_copy(
            held_ref.at[pair % 2],
            out_ref.at[pl.ds(pl.multiple_of(pair * 2 * rows, 2 * rows), 2 * rows)],
            sems.at[pair % 2],
        )

    @pl.loop(0, nl // 2)
    def _(pair):
        @pl.when(pair >= 2)
        def _():
            copy(pair - 2).wait()

        for load in pair_loads(pair):
            load.wait()
        lefts = []
        for i in range(2):
            step = pair * 2 + i
            ay = in_order(
                at_ref, *[ref[:, step].reshape(nb // CORES, nb) for ref in (own_ref, other_ref)]
            )
            lefts.append(jnp.concatenate([left_ref[step], ay], axis=1))
        change = mm3(thrice(jnp.concatenate(lefts, axis=0), True), right_ref[...])
        for i in range(2):
            old_ref = x_ref.at[pl.ds(pl.multiple_of((pair * 2 + i) * rows, rows), rows)]
            new_ref = held_ref.at[pair % 2, pl.ds(i * rows, rows)]

            def put(m, t, value):
                new_ref[pl.ds(t * nm + m, nb, stride=nm * nt), :] = value

            for m in range(nm):
                for t in range(nt):
                    at = m * nb + t * LANES
                    put(
                        m, t,
                        tile(old_ref, m, t, nm, nt) - change[i * nb : (i + 1) * nb, at : at + LANES],
                    )

            @pl.when(at_ref[1] == 0)
            def _():
                band = jnp.zeros((nb, nb), jnp.float32)
                if i == 0:
                    band = jnp.where((pair == 0) & (at_ref[0] == 1), -upper_ref[...], band)
                for t in range(nt):
                    new = band[:, t * LANES : (t + 1) * LANES]
                    if i == 0:
                        keep = (pair == 0) & (at_ref[0] == 0)
                        new = jnp.where(keep, tile(old_ref, 0, t, nm, nt), new)
                    put(0, t, new)

            if i == 0:

                @pl.when((pair == 0) & (at_ref[0] == 0))
                def _():
                    band = jnp.where(at_ref[1] == 1, -upper_ref[...].T, 0.0)
                    for m in range(nm):
                        for t in range(nt):
                            new = jnp.zeros((nb, LANES), jnp.float32)
                            if m == 0:
                                new = band[:, t * LANES : (t + 1) * LANES]
                                new = jnp.where(at_ref[1] == 0, tile(old_ref, m, t, nm, nt), new)
                            put(m, t, new)

        copy(pair).start()

    copy(nl // 2 - 2).wait()
    copy(nl // 2 - 1).wait()


def call(kernel, outs, ins, grid=(), flops=0, moved=1 << 20, scratch=(), out=None):
    return pl.pallas_call(
        kernel,
        grid=grid,
        out_shape=[o(s, jnp.float32) for o, (s, _) in zip(out or [jax.ShapeDtypeStruct] * len(outs), outs)],
        in_specs=ins,
        out_specs=[spec for _, spec in outs],
        scratch_shapes=list(scratch),
        compiler_params=pltpu.CompilerParams(vmem_limit_bytes=24 << 20),
        cost_estimate=pl.CostEstimate(flops=flops, bytes_accessed=moved, transcendentals=0),
    )


def share(piece, axis, count, groups=None):
    copies = jnp.broadcast_to(piece[None], (count,) + piece.shape)
    return lax.all_to_all(copies, axis, 0, 0, axis_index_groups=groups)


def move(block, hops):
    return lax.ppermute(block, "prow", hops)


def near_moves(block):
    return move(block, [(0, 3)]), move(block, [(0, 6)])


def far_moves(block):
    return move(block, [(0, 1), (3, 4)]), move(block, [(0, 7), (3, 2), (6, 5)])


def doubled(block, reach, nz):
    return jnp.concatenate([block, move(block, [(i, i ^ reach) for i in range(nz)])])


def body(hamiltonian):
    nl, nb, nm, _ = hamiltonian.shape
    nt = nb // LANES
    nz = lax.axis_size("prow")
    prow = lax.axis_index("prow")
    pcol = lax.axis_index("pcol")
    core = pcol % CORES
    sub = nb // (CHIPS * CORES)
    nc = nm * nb
    relay = (prow == 0) | (prow == 3) | (prow == 6)
    at = jnp.stack([prow, pcol, core, core * CHIPS + pcol // CORES, relay]).astype(jnp.int32)
    square, wide = (nb, nb), (nb, nc)
    whole = lambda shape: pl.BlockSpec(shape, lambda l: (0,) * len(shape))
    chunk = lambda index: pl.BlockSpec((CHIPS, 1, sub, nb), index)
    barrier = lax.optimization_barrier

    x = hamiltonian.reshape(nl, nb, nm, nt, LANES).transpose(0, 1, 3, 2, 4)
    x = x.reshape(nl * nb * nt * nm, LANES)
    x_rows = nb * nt * nm
    x_spec = pl.BlockSpec((x_rows, LANES), lambda l: (l, 0))

    first_rows = x[:x_rows]

    packet_shape = (CORES, CHIPS, nl + 1, sub, nb)
    packet = call(
        functools.partial(pack_kernel, nm, nt),
        [(packet_shape, whole(packet_shape))],
        [SMEM, HBM],
        grid=(nl,),
        flops=2 * 10**10,
        moved=6 << 20,
        scratch=[
            pltpu.VMEM(square, jnp.float32),
            pltpu.VMEM((nl, x_rows, LANES), jnp.float32),
            pltpu.SemaphoreType.DMA((nl,)),
        ],
    )(at, pltpu.with_memory_space_constraint(x, pltpu.HBM))[0]
    outgoing = jnp.where(core == 0, packet[0], lax.ppermute(packet[1], "pcol", [(0, 1)]))
    near = near_moves(first_rows)
    mine = lax.all_to_all(outgoing, "pcol", 0, 0, axis_index_groups=PLANE)[0]
    near, mine = barrier((near, mine))
    p_cols = jnp.where(prow == 0, first_rows, near[0] + near[1])
    stacked = share(jnp.stack([mine[nl], mine[0]]), "prow", nz)
    summed = jnp.stack([jnp.sum(stacked[:, 0], axis=0), stacked[1, 1]])
    small = share(summed, "pcol", CHIPS, PLANE)
    p_cols, small, mine = barrier((p_cols, small, mine))
    far = far_moves(p_cols)
    other_small = lax.ppermute(small, "pcol", SWAP)
    small_half = lambda i: (small[:, i], other_small[:, i])
    inv, upper, inv_kept, inv_t = call(
        factor_kernel,
        [(square, VMEM)] + [(square, HBM)] * 3,
        [SMEM, VMEM, VMEM],
        flops=10**10,
        out=[jax.ShapeDtypeStruct] + [pltpu.HBM] * 3,
        scratch=[pltpu.VMEM(square, jnp.float32)] * 2 + [pltpu.SemaphoreType.DMA((3,))],
    )(at, *small_half(0))
    own_p = share(mine[:nl], "pcol", CHIPS, PLANE)

    half_shape = (nl, nb // CORES, nb)
    row_spec = chunk(lambda l: (0, l, 0, 0))
    keep, send, y_cols = call(
        functools.partial(apply_kernel, nm, nt),
        [(half_shape, VMEM), (half_shape, HBM), (wide, HBM)],
        [SMEM, VMEM, HBM, HBM, HBM, VMEM],
        out=[jax.ShapeDtypeStruct, pltpu.HBM, pltpu.HBM],
        scratch=[pltpu.VMEM((x_rows, LANES), jnp.float32)] * 3
        + [
            pltpu.VMEM(wide, jnp.float32),
            pltpu.VMEM(half_shape, jnp.float32),
            pltpu.SemaphoreType.DMA((3,)),
            pltpu.SemaphoreType.DMA,
            pltpu.SemaphoreType.DMA((nl,)),
        ],
        flops=12 * nl * nb**2 * nc,
        moved=9 << 20,
    )(at, x, *[pltpu.with_memory_space_constraint(a, pltpu.HBM) for a in (p_cols, *far)], inv)
    keep, send, own_p = barrier((keep, send, own_p))
    other_p = lax.ppermute(own_p, "pcol", SWAP)
    parts = (keep + lax.ppermute(send, "pcol", SWAP)).reshape(nl, CHIPS, sub, nb).transpose(1, 0, 2, 3)
    parts = lax.all_to_all(parts, "pcol", 0, 0, axis_index_groups=PLANE)
    y_rows, slab = call(
        rows_kernel,
        [((nl, nb, nb), pl.BlockSpec((1, nb, nb), lambda l: (l, 0, 0))),
         ((sub, nl * nb), pl.BlockSpec((sub, nb), lambda l: (0, l)))],
        [SMEM, row_spec, row_spec, whole(square)],
        grid=(nl,),
        flops=5 * 10**9,
        moved=6 << 20,
        scratch=[pltpu.VMEM(square, jnp.float32)],
        out=[pltpu.HBM, jax.ShapeDtypeStruct],
    )(at, own_p, other_p, inv_t)
    parts, slab = barrier((parts, slab))
    piece = jnp.sum(parts, axis=0)
    own = share(piece, "pcol", CHIPS, PLANE)
    mixer = call(
        mixer_kernel,
        [(square, VMEM)],
        [SMEM] + [chunk(lambda l: (0, 1, 0, 0))] * 2 + [VMEM, pl.BlockSpec(memory_space=pl.ANY)],
        grid=(1,),
        flops=10**10,
    )(at, small, other_small, inv_kept, parts)[0]
    four = doubled(doubled(piece[None], 4, nz), 2, nz)
    own, mixer, four = barrier((own, mixer, four))
    other = lax.ppermute(own, "pcol", SWAP)

    ay_halves = [pltpu.with_memory_space_constraint(a, pltpu.HBM) for a in (own, other)]

    copies = call(
        proj_kernel,
        [((nz, sub, nb), VMEM)],
        [SMEM, VMEM, HBM, HBM],
        scratch=[pltpu.VMEM(own.shape, jnp.float32)] * 2 + [pltpu.SemaphoreType.DMA((nl // 2,))] * 2,
        flops=10**9,
        moved=4 << 20,
    )(at, slab, *ay_halves)[0]
    pieces = lax.all_to_all(copies, "prow", 0, 0)
    more = move(four, [(i, i ^ 1) for i in range(nz)])
    more, pieces = barrier((more, pieces))
    lines = CHIPS * CORES
    routed = call(
        functools.partial(route_kernel, nm),
        [((lines, nm + 1, sub, nb), VMEM)],
        [SMEM] + [VMEM] * 3,
        flops=10**8,
    )(at, four, more, pieces)[0]
    routed = lax.all_to_all(routed, "pcol", 0, 0)
    out = call(
        functools.partial(update_kernel, nm, nt),
        [(x.shape, HBM)],
        [SMEM] + [HBM] * 4 + [VMEM] * 2 + [HBM] * 2,
        flops=12 * nl * nb**2 * nc,
        moved=12 << 20,
        scratch=[
            pltpu.VMEM((6 * nb, nc), jnp.bfloat16),
            pltpu.VMEM((2, 2 * x_rows, LANES), jnp.float32),
            pltpu.VMEM(wide, jnp.float32),
            pltpu.VMEM(square, jnp.float32),
            pltpu.VMEM(x.shape, jnp.float32),
            pltpu.VMEM((nl, nb, nb), jnp.float32),
            pltpu.VMEM(own.shape, jnp.float32),
            pltpu.VMEM(own.shape, jnp.float32),
            pltpu.SemaphoreType.DMA((2,)),
            pltpu.SemaphoreType.DMA((2,)),
        ]
        + [pltpu.SemaphoreType.DMA((nl // 2,))] * 4,
    )(at, pltpu.with_memory_space_constraint(x, pltpu.HBM), y_rows, *ay_halves, routed.reshape(CHIPS, CORES, nm + 1, sub, nb), mixer, y_cols, upper)[0]
    out = out.reshape(nl, nb, nt, nm, LANES).transpose(0, 1, 3, 2, 4)
    return out.reshape(hamiltonian.shape)


def solution(mesh):
    return jax.shard_map(
        body,
        mesh=mesh,
        in_specs=(P(None, "prow", None, "pcol"),),
        out_specs=P(None, "prow", None, "pcol"),
        check_vma=False,
    )
```

```python
import functools
import jax
import jax.numpy as jnp
from jax import lax
from jax.experimental import pallas as pl
from jax.experimental.pallas import tpu as pltpu
from jax.sharding import PartitionSpec as P

HP = lax.Precision.HIGHEST
XS, YS, CORES = 4, 4, 2
CHIPS = XS * YS
LANES = 128
BASE = 64
GROUP = 8
PLANE = [[q * CORES + k for q in range(CHIPS)] for k in range(CORES)]
SWAP = [(i, i ^ 1) for i in range(CHIPS * CORES)]
VMEM = pl.BlockSpec(memory_space=pltpu.VMEM)
SMEM = pl.BlockSpec(memory_space=pltpu.SMEM)
HBM = pl.BlockSpec(memory_space=pltpu.HBM)


def mm(a, b):
    return jnp.dot(a, b, precision=HP, preferred_element_type=jnp.float32)


def mm_tn(a, b):
    return lax.dot_general(a, b, (((0,), (0,)), ((), ())), precision=HP, preferred_element_type=jnp.float32)


def mm_nt(a, b):
    return lax.dot_general(a, b, (((1,), (1,)), ((), ())), precision=HP, preferred_element_type=jnp.float32)


def eliminate(block, jordan):
    n = block.shape[0]
    eye = (lax.broadcasted_iota(jnp.int32, (n, n), 0) == lax.broadcasted_iota(jnp.int32, (n, n), 1))
    wide = jnp.concatenate([block, eye.astype(jnp.float32)], axis=1)
    shape = (GROUP, 2 * n)
    groups = n // GROUP
    at = lax.broadcasted_iota(jnp.int32, shape, 0)
    w = [wide[g * GROUP : (g + 1) * GROUP] for g in range(groups)]
    for p in range(groups):
        live = [g for g in range(groups) if jordan or g >= p]
        cols = {
            g: [
                jnp.broadcast_to(w[g][:, p * GROUP + b : p * GROUP + b + 1], shape)
                for b in range(GROUP)
            ]
            for g in live
        }
        for a in range(GROUP):
            inv = 1.0 / cols[p][a][a : a + 1]
            row = w[p][a : a + 1]
            heads = [cols[p][b][a : a + 1] for b in range(GROUP)]
            for g in live:
                m = cols[g][a] * inv
                if g == p:
                    m = jnp.where(at != a if jordan else at > a, m, 0.0)
                for b in range(a + 1, GROUP):
                    cols[g][b] = cols[g][b] - m * heads[b]
                w[g] = w[g] - m * row
    return jnp.concatenate(w, axis=0)


def diagonal(wide):
    n = wide.shape[0]
    shape = wide.shape
    eye = lax.broadcasted_iota(jnp.int32, shape, 0) == lax.broadcasted_iota(jnp.int32, shape, 1)
    return jnp.sum(jnp.where(eye, wide, 0.0), axis=1, keepdims=True)


def factor(a):
    n = a.shape[0]
    if n <= BASE:
        wide = eliminate(a, False)
        wide = wide * (1.0 / jnp.sqrt(diagonal(wide)))
        left = wide[:, :n]
        upper = lax.broadcasted_iota(jnp.int32, (n, n), 0) <= lax.broadcasted_iota(jnp.int32, (n, n), 1)
        return jnp.where(upper, left, 0.0), wide[:, n:]
    h = n // 2
    u11, i11 = factor(a[:h, :h])
    u12 = mm(i11, a[:h, h:])
    u22, i22 = factor(a[h:, h:] - mm_tn(u12, u12))
    i21 = -mm(i22, mm_tn(u12, i11))
    zero = jnp.zeros((h, h), jnp.float32)
    upper = jnp.concatenate([jnp.concatenate([u11, u12], 1), jnp.concatenate([zero, u22], 1)], 0)
    inv = jnp.concatenate([jnp.concatenate([i11, zero], 1), jnp.concatenate([i21, i22], 1)], 0)
    return upper, inv


def inverse(a):
    n = a.shape[0]
    if n <= BASE:
        wide = eliminate(a, True)
        return (wide * (1.0 / diagonal(wide)))[:, n:]
    h = n // 2
    i11 = inverse(a[:h, :h])
    x = mm(i11, a[:h, h:])
    y = mm(a[h:, :h], i11)
    s = inverse(a[h:, h:] - mm(a[h:, :h], x))
    xs = mm(x, s)
    top = jnp.concatenate([i11 + mm(xs, y), -xs], 1)
    return jnp.concatenate([top, jnp.concatenate([-mm(s, y), s], 1)], 0)


def halves(a):
    high = a.astype(jnp.bfloat16)
    return high, (a - high.astype(jnp.float32)).astype(jnp.bfloat16)


def thrice(a, left):
    high, low = halves(a)
    return jnp.concatenate([high, low, high] if left else [high, high, low], axis=1 if left else 0)


def mm3(left, right):
    return jnp.dot(left, right, preferred_element_type=jnp.float32)


def identity(n):
    rows = lax.broadcasted_iota(jnp.int32, (n, n), 0)
    return (rows == lax.broadcasted_iota(jnp.int32, (n, n), 1)).astype(jnp.float32)


def tile(ref, m, t, nm, nt):
    return ref[pl.ds(t * nm + m, ref.shape[0] // (nm * nt), stride=nm * nt), :]


def fetched(step, x_ref, held_ref, sems):
    rows = held_ref.shape[1]
    copy = lambda i: pltpu.make_async_copy(
        x_ref.at[pl.ds(pl.multiple_of(i * rows, rows), rows)], held_ref.at[i], sems.at[i]
    )

    @pl.when(step == 0)
    def _():
        for i in range(held_ref.shape[0]):
            copy(i).start()

    copy(step).wait()
    return held_ref.at[step]


def in_order(at_ref, own, other):
    first = at_ref[2] == 0
    return jnp.concatenate([jnp.where(first, own, other), jnp.where(first, other, own)], axis=0)


def rows_of(ref):
    return ref[...].reshape(-1, ref.shape[-1])


def pack_kernel(nm, nt, at_ref, x_ref, packet_ref, gram_ref, held_ref, sems):
    step = pl.program_id(0)
    x_ref = fetched(step, x_ref, held_ref, sems)
    panel = jnp.concatenate([tile(x_ref, 0, t, nm, nt) for t in range(nt)], axis=1)
    panel = jnp.where((step == 0) & (at_ref[0] == 0), 0.0, panel)
    last = packet_ref.shape[2] - 1
    packet_ref[:, :, pl.ds(step, 1)] = panel.reshape(CORES, CHIPS, 1, *packet_ref.shape[3:])
    more = mm_tn(panel, panel)

    @pl.when(step == 0)
    def _():
        gram_ref[...] = more

    @pl.when(step > 0)
    def _():
        gram_ref[...] += more

    @pl.when(step == last - 1)
    def _():
        packet_ref[:, :, last] = gram_ref[...].reshape(CORES, CHIPS, *packet_ref.shape[3:])


def factor_kernel(
    at_ref, own_ref, other_ref, inv_ref, upper_hbm, inv_hbm, inv_t_hbm, upper_ref, inv_t_ref, sems
):
    upper, inv = factor(in_order(at_ref, rows_of(own_ref), rows_of(other_ref)))
    upper_ref[...] = upper
    inv_ref[...] = inv
    inv_t_ref[...] = inv.T
    stores = [
        pltpu.make_async_copy(src, dst, sems.at[i])
        for i, (src, dst) in enumerate(
            ((upper_ref, upper_hbm), (inv_ref, inv_hbm), (inv_t_ref, inv_t_hbm))
        )
    ]
    for store in stores:
        store.start()
    for store in stores:
        store.wait()


def mixer_kernel(at_ref, own_ref, other_ref, inv_ref, after_ref, mixer_ref):
    top = in_order(at_ref, rows_of(own_ref), rows_of(other_ref))
    mixer_ref[...] = inverse(identity(top.shape[0]) + mm_nt(inv_ref[...], top))


def rows_kernel(at_ref, own_ref, other_ref, inv_t_ref, y_ref, slab_ref, flip_ref):
    y = mm(in_order(at_ref, rows_of(own_ref), rows_of(other_ref)), inv_t_ref[...])
    y += jnp.where((pl.program_id(0) == 0) & (at_ref[0] == 1), identity(y.shape[0]), 0.0)
    y_ref[0] = y
    flip_ref[...] = y.T
    deep = slab_ref.shape[0]
    slab_ref[...] = flip_ref[pl.ds(pl.multiple_of(at_ref[3] * deep, deep), deep), :]


def apply_kernel(
    nm, nt, at_ref, x_ref, top_hbm, far_hbm, more_hbm, inv_ref, keep_ref, send_hbm, y_hbm,
    top_ref, far_ref, more_ref, y_ref, send_ref, in_sems, out_sem, send_sems,
):
    nl, hb, nb = keep_ref.shape
    rows = nb * nt * nm
    loads = [
        pltpu.make_async_copy(src, dst, in_sems.at[i])
        for i, (src, dst) in enumerate(
            ((top_hbm, top_ref), (far_hbm, far_ref), (more_hbm, more_ref))
        )
    ]
    for load in loads:
        load.start()
    for load in loads:
        load.wait()
    for m in range(nm):
        panel = jnp.concatenate(
            [
                jnp.where(
                    at_ref[4] == 1,
                    tile(top_ref, m, t, nm, nt),
                    tile(far_ref, m, t, nm, nt) + tile(more_ref, m, t, nm, nt),
                )
                for t in range(nt)
            ],
            axis=1,
        )
        if m == 0:
            panel = jnp.where(at_ref[1] == 0, 0.0, panel)
        y = mm(inv_ref[...], panel)
        if m == 0:
            y += jnp.where(at_ref[1] == 1, identity(nb), 0.0)
        y_ref[:, m * nb : (m + 1) * nb] = y
    store = pltpu.make_async_copy(y_ref, y_hbm, out_sem)
    store.start()
    right = thrice(y_ref[...].T, False)
    first = at_ref[2] == 0
    send = lambda step: pltpu.make_async_copy(send_ref.at[step], send_hbm.at[step], send_sems.at[step])

    @pl.loop(0, nl // 2)
    def _(pair):
        blocks = []
        for i in range(2):
            step = pair * 2 + i
            rows_ref = x_ref.at[pl.ds(pl.multiple_of(step * rows, rows), rows)]
            blocks.append(
                jnp.concatenate(
                    [tile(rows_ref, m, t, nm, nt) for m in range(nm) for t in range(nt)], axis=1
                )
            )
        both = mm3(thrice(jnp.concatenate(blocks, axis=0), True), right)
        for i in range(2):
            step = pair * 2 + i
            part = both[i * nb : (i + 1) * nb]
            if i == 0:
                part = jnp.where((pair == 0) & (at_ref[0] == 0), 0.0, part)
            keep_ref[step] = jnp.where(first, part[:hb], part[hb:])
            send_ref[step] = jnp.where(first, part[hb:], part[:hb])
            send(step).start()

    for step in range(nl):
        send(step).wait()
    store.wait()


def half_loads(pair, own_hbm, other_hbm, own_ref, other_ref, own_sems, other_sems):
    two = pl.ds(pair * 2, 2)
    return (
        pltpu.make_async_copy(own_hbm.at[:, two], own_ref.at[:, two], own_sems.at[pair]),
        pltpu.make_async_copy(other_hbm.at[:, two], other_ref.at[:, two], other_sems.at[pair]),
    )


def proj_kernel(
    at_ref, slab_ref, own_hbm, other_hbm, copies_ref, own_ref, other_ref, own_sems, other_sems
):
    nl = own_ref.shape[1]
    nb = own_ref.shape[3]
    loads = [
        half_loads(p, own_hbm, other_hbm, own_ref, other_ref, own_sems, other_sems)
        for p in range(nl // 2)
    ]
    for pair in loads:
        for load in pair:
            load.start()
    total = jnp.zeros(copies_ref.shape[1:], jnp.float32)
    for step in range(nl):
        if step % 2 == 0:
            for load in loads[step // 2]:
                load.wait()
        ay = in_order(
            at_ref, *[ref[:, step].reshape(nb // CORES, nb) for ref in (own_ref, other_ref)]
        )
        total += mm(slab_ref[:, step * nb : (step + 1) * nb], ay)
    for i in range(copies_ref.shape[0]):
        copies_ref[i] = total


def route_kernel(nm, at_ref, four_ref, more_ref, pieces_ref, out_ref):
    nz, sub, nb = pieces_ref.shape
    total = jnp.sum(pieces_ref[...], axis=0)
    deep = four_ref.shape[1] // nm
    for z in range(nz):
        bits = z ^ at_ref[0]
        place = (bits & 2) | ((bits >> 2) & 1)

        def put(ref):
            for m in range(nm):
                for i in range(deep):
                    out_ref[i * nz + z, m] = ref[place, m * deep + i]

        @pl.when((bits & 1) == 0)
        def _():
            put(four_ref)

        @pl.when((bits & 1) == 1)
        def _():
            put(more_ref)

    for i in range(out_ref.shape[0]):
        out_ref[i, nm] = total


def update_kernel(
    nm, nt, at_ref, x_hbm, left_hbm, own_hbm, other_hbm, rows_ref, mixer_ref, y_hbm, upper_hbm,
    out_ref, right_ref, held_ref, y_ref, upper_ref, x_ref, left_ref, own_ref, other_ref,
    sems, in_sems, x_sems, left_sems, own_sems, other_sems,
):
    nb = mixer_ref.shape[0]
    nl = left_ref.shape[0]
    rows = nb * nt * nm

    def pair_loads(pair):
        at = pl.ds(pl.multiple_of(pair * 2 * rows, 2 * rows), 2 * rows)
        two = pl.ds(pair * 2, 2)
        return (
            pltpu.make_async_copy(x_hbm.at[at], x_ref.at[at], x_sems.at[pair]),
            pltpu.make_async_copy(left_hbm.at[two], left_ref.at[two], left_sems.at[pair]),
        ) + half_loads(pair, own_hbm, other_hbm, own_ref, other_ref, own_sems, other_sems)

    loads = [
        pltpu.make_async_copy(src, dst, in_sems.at[i])
        for i, (src, dst) in enumerate(((y_hbm, y_ref), (upper_hbm, upper_ref)))
    ]
    for load in loads:
        load.start()
    for pair in range(nl // 2):
        for load in pair_loads(pair):
            load.start()
    mixer = mixer_ref[...]

    def gathered(m):
        return jnp.concatenate(
            [rows_ref[:, k, m].reshape(nb // CORES, nb) for k in range(CORES)], axis=0
        )

    core = mm(mm_tn(mixer, gathered(nm)), mixer)
    z = lax.dot_general(
        mixer,
        jnp.concatenate([gathered(m) for m in range(nm)], axis=0),
        (((0,), (1,)), ((), ())),
        precision=HP,
        preferred_element_type=jnp.float32,
    )
    for load in loads:
        load.wait()
    y = y_ref[...]
    right_ref[...] = thrice(jnp.concatenate([z - mm_tn(core, y), mm(mixer, y)], axis=0), False)

    def copy(pair):
        return pltpu.make_async_copy(
            held_ref.at[pair % 2],
            out_ref.at[pl.ds(pl.multiple_of(pair * 2 * rows, 2 * rows), 2 * rows)],
            sems.at[pair % 2],
        )

    @pl.loop(0, nl // 2)
    def _(pair):
        @pl.when(pair >= 2)
        def _():
            copy(pair - 2).wait()

        for load in pair_loads(pair):
            load.wait()
        lefts = []
        for i in range(2):
            step = pair * 2 + i
            ay = in_order(
                at_ref, *[ref[:, step].reshape(nb // CORES, nb) for ref in (own_ref, other_ref)]
            )
            lefts.append(jnp.concatenate([left_ref[step], ay], axis=1))
        change = mm3(thrice(jnp.concatenate(lefts, axis=0), True), right_ref[...])
        for i in range(2):
            old_ref = x_ref.at[pl.ds(pl.multiple_of((pair * 2 + i) * rows, rows), rows)]
            new_ref = held_ref.at[pair % 2, pl.ds(i * rows, rows)]

            def put(m, t, value):
                new_ref[pl.ds(t * nm + m, nb, stride=nm * nt), :] = value

            for m in range(nm):
                for t in range(nt):
                    at = m * nb + t * LANES
                    put(
                        m, t,
                        tile(old_ref, m, t, nm, nt) - change[i * nb : (i + 1) * nb, at : at + LANES],
                    )

            @pl.when(at_ref[1] == 0)
            def _():
                band = jnp.zeros((nb, nb), jnp.float32)
                if i == 0:
                    band = jnp.where((pair == 0) & (at_ref[0] == 1), -upper_ref[...], band)
                for t in range(nt):
                    new = band[:, t * LANES : (t + 1) * LANES]
                    if i == 0:
                        keep = (pair == 0) & (at_ref[0] == 0)
                        new = jnp.where(keep, tile(old_ref, 0, t, nm, nt), new)
                    put(0, t, new)

            if i == 0:

                @pl.when((pair == 0) & (at_ref[0] == 0))
                def _():
                    band = jnp.where(at_ref[1] == 1, -upper_ref[...].T, 0.0)
                    for m in range(nm):
                        for t in range(nt):
                            new = jnp.zeros((nb, LANES), jnp.float32)
                            if m == 0:
                                new = band[:, t * LANES : (t + 1) * LANES]
                                new = jnp.where(at_ref[1] == 0, tile(old_ref, m, t, nm, nt), new)
                            put(m, t, new)

        copy(pair).start()

    copy(nl // 2 - 2).wait()
    copy(nl // 2 - 1).wait()


def call(kernel, outs, ins, grid=(), flops=0, moved=1 << 20, scratch=(), out=None):
    return pl.pallas_call(
        kernel,
        grid=grid,
        out_shape=[o(s, jnp.float32) for o, (s, _) in zip(out or [jax.ShapeDtypeStruct] * len(outs), outs)],
        in_specs=ins,
        out_specs=[spec for _, spec in outs],
        scratch_shapes=list(scratch),
        compiler_params=pltpu.CompilerParams(vmem_limit_bytes=24 << 20),
        cost_estimate=pl.CostEstimate(flops=flops, bytes_accessed=moved, transcendentals=0),
    )


def share(piece, axis, count, groups=None):
    copies = jnp.broadcast_to(piece[None], (count,) + piece.shape)
    return lax.all_to_all(copies, axis, 0, 0, axis_index_groups=groups)


def move(block, hops):
    return lax.ppermute(block, "prow", hops)


def near_moves(block):
    return move(block, [(0, 3)]), move(block, [(0, 6)])


def far_moves(block):
    return move(block, [(0, 1), (3, 4)]), move(block, [(0, 7), (3, 2), (6, 5)])


def doubled(block, reach, nz):
    return jnp.concatenate([block, move(block, [(i, i ^ reach) for i in range(nz)])])


def body(hamiltonian):
    nl, nb, nm, _ = hamiltonian.shape
    nt = nb // LANES
    nz = lax.axis_size("prow")
    prow = lax.axis_index("prow")
    pcol = lax.axis_index("pcol")
    core = pcol % CORES
    sub = nb // (CHIPS * CORES)
    nc = nm * nb
    relay = (prow == 0) | (prow == 3) | (prow == 6)
    at = jnp.stack([prow, pcol, core, core * CHIPS + pcol // CORES, relay]).astype(jnp.int32)
    square, wide = (nb, nb), (nb, nc)
    whole = lambda shape: pl.BlockSpec(shape, lambda l: (0,) * len(shape))
    chunk = lambda index: pl.BlockSpec((CHIPS, 1, sub, nb), index)
    barrier = lax.optimization_barrier

    x = hamiltonian.reshape(nl, nb, nm, nt, LANES).transpose(0, 1, 3, 2, 4)
    x = x.reshape(nl * nb * nt * nm, LANES)
    x_rows = nb * nt * nm
    x_spec = pl.BlockSpec((x_rows, LANES), lambda l: (l, 0))

    first_rows = x[:x_rows]

    packet_shape = (CORES, CHIPS, nl + 1, sub, nb)
    packet = call(
        functools.partial(pack_kernel, nm, nt),
        [(packet_shape, whole(packet_shape))],
        [SMEM, HBM],
        grid=(nl,),
        flops=2 * 10**10,
        moved=6 << 20,
        scratch=[
            pltpu.VMEM(square, jnp.float32),
            pltpu.VMEM((nl, x_rows, LANES), jnp.float32),
            pltpu.SemaphoreType.DMA((nl,)),
        ],
    )(at, pltpu.with_memory_space_constraint(x, pltpu.HBM))[0]
    outgoing = jnp.where(core == 0, packet[0], lax.ppermute(packet[1], "pcol", [(0, 1)]))
    near = near_moves(first_rows)
    mine = lax.all_to_all(outgoing, "pcol", 0, 0, axis_index_groups=PLANE)[0]
    near, mine = barrier((near, mine))
    p_cols = jnp.where(prow == 0, first_rows, near[0] + near[1])
    stacked = share(jnp.stack([mine[nl], mine[0]]), "prow", nz)
    summed = jnp.stack([jnp.sum(stacked[:, 0], axis=0), stacked[1, 1]])
    small = share(summed, "pcol", CHIPS, PLANE)
    p_cols, small, mine = barrier((p_cols, small, mine))
    far = far_moves(p_cols)
    other_small = lax.ppermute(small, "pcol", SWAP)
    small_half = lambda i: (small[:, i], other_small[:, i])
    inv, upper, inv_kept, inv_t = call(
        factor_kernel,
        [(square, VMEM)] + [(square, HBM)] * 3,
        [SMEM, VMEM, VMEM],
        flops=10**10,
        out=[jax.ShapeDtypeStruct] + [pltpu.HBM] * 3,
        scratch=[pltpu.VMEM(square, jnp.float32)] * 2 + [pltpu.SemaphoreType.DMA((3,))],
    )(at, *small_half(0))
    own_p = share(mine[:nl], "pcol", CHIPS, PLANE)

    half_shape = (nl, nb // CORES, nb)
    row_spec = chunk(lambda l: (0, l, 0, 0))
    keep, send, y_cols = call(
        functools.partial(apply_kernel, nm, nt),
        [(half_shape, VMEM), (half_shape, HBM), (wide, HBM)],
        [SMEM, VMEM, HBM, HBM, HBM, VMEM],
        out=[jax.ShapeDtypeStruct, pltpu.HBM, pltpu.HBM],
        scratch=[pltpu.VMEM((x_rows, LANES), jnp.float32)] * 3
        + [
            pltpu.VMEM(wide, jnp.float32),
            pltpu.VMEM(half_shape, jnp.float32),
            pltpu.SemaphoreType.DMA((3,)),
            pltpu.SemaphoreType.DMA,
            pltpu.SemaphoreType.DMA((nl,)),
        ],
        flops=12 * nl * nb**2 * nc,
        moved=9 << 20,
    )(at, x, *[pltpu.with_memory_space_constraint(a, pltpu.HBM) for a in (p_cols, *far)], inv)
    keep, send, own_p = barrier((keep, send, own_p))
    parts = (keep + lax.ppermute(send, "pcol", SWAP)).reshape(nl, CHIPS, sub, nb).transpose(1, 0, 2, 3)
    parts, own_p = barrier((parts, own_p))
    other_p = lax.ppermute(own_p, "pcol", SWAP)
    parts = lax.all_to_all(parts, "pcol", 0, 0, axis_index_groups=PLANE)
    y_rows, slab = call(
        rows_kernel,
        [((nl, nb, nb), pl.BlockSpec((1, nb, nb), lambda l: (l, 0, 0))),
         ((sub, nl * nb), pl.BlockSpec((sub, nb), lambda l: (0, l)))],
        [SMEM, row_spec, row_spec, whole(square)],
        grid=(nl,),
        flops=5 * 10**9,
        moved=6 << 20,
        scratch=[pltpu.VMEM(square, jnp.float32)],
        out=[pltpu.HBM, jax.ShapeDtypeStruct],
    )(at, own_p, other_p, inv_t)
    parts, slab = barrier((parts, slab))
    piece = jnp.sum(parts, axis=0)
    own = share(piece, "pcol", CHIPS, PLANE)
    mixer = call(
        mixer_kernel,
        [(square, VMEM)],
        [SMEM] + [chunk(lambda l: (0, 1, 0, 0))] * 2 + [VMEM, pl.BlockSpec(memory_space=pl.ANY)],
        grid=(1,),
        flops=10**10,
    )(at, small, other_small, inv_kept, parts)[0]
    four = doubled(doubled(piece[None], 4, nz), 2, nz)
    own, mixer, four = barrier((own, mixer, four))
    other = lax.ppermute(own, "pcol", SWAP)

    ay_halves = [pltpu.with_memory_space_constraint(a, pltpu.HBM) for a in (own, other)]

    copies = call(
        proj_kernel,
        [((nz, sub, nb), VMEM)],
        [SMEM, VMEM, HBM, HBM],
        scratch=[pltpu.VMEM(own.shape, jnp.float32)] * 2 + [pltpu.SemaphoreType.DMA((nl // 2,))] * 2,
        flops=10**9,
        moved=4 << 20,
    )(at, slab, *ay_halves)[0]
    pieces = lax.all_to_all(copies, "prow", 0, 0)
    more = move(four, [(i, i ^ 1) for i in range(nz)])
    more, pieces = barrier((more, pieces))
    lines = CHIPS * CORES
    routed = call(
        functools.partial(route_kernel, nm),
        [((lines, nm + 1, sub, nb), VMEM)],
        [SMEM] + [VMEM] * 3,
        flops=10**8,
    )(at, four, more, pieces)[0]
    routed = lax.all_to_all(routed, "pcol", 0, 0)
    out = call(
        functools.partial(update_kernel, nm, nt),
        [(x.shape, HBM)],
        [SMEM] + [HBM] * 4 + [VMEM] * 2 + [HBM] * 2,
        flops=12 * nl * nb**2 * nc,
        moved=12 << 20,
        scratch=[
            pltpu.VMEM((6 * nb, nc), jnp.bfloat16),
            pltpu.VMEM((2, 2 * x_rows, LANES), jnp.float32),
            pltpu.VMEM(wide, jnp.float32),
            pltpu.VMEM(square, jnp.float32),
            pltpu.VMEM(x.shape, jnp.float32),
            pltpu.VMEM((nl, nb, nb), jnp.float32),
            pltpu.VMEM(own.shape, jnp.float32),
            pltpu.VMEM(own.shape, jnp.float32),
            pltpu.SemaphoreType.DMA((2,)),
            pltpu.SemaphoreType.DMA((2,)),
        ]
        + [pltpu.SemaphoreType.DMA((nl // 2,))] * 4,
    )(at, pltpu.with_memory_space_constraint(x, pltpu.HBM), y_rows, *ay_halves, routed.reshape(CHIPS, CORES, nm + 1, sub, nb), mixer, y_cols, upper)[0]
    out = out.reshape(nl, nb, nt, nm, LANES).transpose(0, 1, 3, 2, 4)
    return out.reshape(hamiltonian.shape)


def solution(mesh):
    return jax.shard_map(
        body,
        mesh=mesh,
        in_specs=(P(None, "prow", None, "pcol"),),
        out_specs=P(None, "prow", None, "pcol"),
        check_vma=False,
    )
```
